32 devices in a mesh: dp: 8 (over z, x), tensor: 4 (over y, core).
Axes of the slice: x: 2, y: 2, z: 4, core: 2. Of those that a mesh axis runs over, the one named last changes fastest.
Arguments:
- image_tokens: bfloat16 [12608, 768], P('dp'), may hold values from -6 to 6
- image_count: int32 [8], P('dp'), may hold values from 1 to 8, as said below
- expert_routes: int32 [12608, 2], P('dp'), may hold values from 0 to 7, all different within a row; in each aligned block of 1576 rows (0 to 1575, 1576 to 3151, ...) at most 396 rows name the same one
- out_cotangent: bfloat16 [12608, 768], P('dp'), may hold values from -6 to 6
- norm_gains: float32 [2, 2, 768], replicated, may hold values from 0.5 to 1.5
- attn_qkv: bfloat16 [2, 3, 768, 768], P(None, None, None, 'tensor'), may hold values from -0.21875 to 0.21875
- attn_proj: bfloat16 [2, 768, 768], P(None, 'tensor'), may hold values from -2 to 2
- dense_up: bfloat16 [768, 3072], P(None, 'tensor'), may hold values from -0.21875 to 0.21875
- dense_down: bfloat16 [3072, 768], P('tensor'), may hold values from -0.109375 to 0.109375
- router_weight: float32 [768, 8], replicated, may hold values from -0.15625 to 0.15625
- expert_up: bfloat16 [8, 768, 3072], P('dp', None, 'tensor'), may hold values from -0.21875 to 0.21875
- expert_down: bfloat16 [8, 3072, 768], P('dp', 'tensor'), may hold values from -1.25 to 1.25
Outputs:
- block_output: bfloat16 [12608, 768], P('dp')
- input_grad: float32 [12608, 768], P('dp')
- gains_grad: float32 [2, 2, 768], replicated
- qkv_grad: float32 [2, 3, 768, 768], P(None, None, None, 'tensor')
- proj_grad: float32 [2, 768, 768], P(None, 'tensor')
- up_grad: float32 [768, 3072], P(None, 'tensor')
- down_grad: float32 [3072, 768], P('tensor')
- router_grad: float32 [768, 8], replicated
- expert_up_grad: float32 [8, 768, 3072], P('dp', None, 'tensor')
- expert_down_grad: float32 [8, 3072, 768], P('dp', 'tensor')
The draws below stay inside these ranges and needn't reach their ends.
Inputs may be any that keep to these rules, and one draw needn't show every extreme that they name: `expert_routes`: each row names two different experts. Among the rows of one index of dp no expert is named more than 396 times, a bound that some block reaches. Index d of dp holds image_count[d] live images in its first slots, the others are padding whose tokens go to no expert; some index has all 8 slots live.
All inputs are finite; a program needn't handle non-finite values.
Results may differ from the reference program's by a relative error of at most 0.028.
The reference program's roundings to bfloat16 on the way count: a program that leaves them out, or rounds other values in their place, can miss the bound.
Values may be sent and summed in bfloat16 or wider, within the bound.
No kernel may reach another device: no remote copies, remote signals or barrier semaphores. Data moves between devices by JAX's collectives and lax.ppermute only.
A program may use at most 256 MiB of HBM per device.

```python
import math
import jax
import jax.numpy as jnp
import numpy as np
from jax import lax

D = 768
HEADS = 12
HD = 64
FF = 3072
SEQ = 197
LAYERS = 2
IMG_SLOTS = 8
EXPERTS = 8
TOK_DEV = 1576
TOKENS = 12608
CAP = 396
N_DP = 8


def draw_image_count(key, part):
    key = jax.random.fold_in(key, 7)
    count_key, full_key = jax.random.split(key)
    counts = jax.random.randint(count_key, (N_DP,), 1, IMG_SLOTS + 1)
    chosen = jax.random.randint(full_key, (), 0, N_DP)
    return jnp.where(jnp.arange(N_DP) == chosen, IMG_SLOTS, counts).astype(jnp.int32)


def levels(own_key, extent, shards, low, largest):
    factor_of = 1.0
    for axis_at, parts in shards:
        heights = jax.random.uniform(jax.random.fold_in(jax.random.fold_in(own_key, 6), axis_at), (parts,), jnp.float32, low / len(shards), largest / len(shards))
        factor_of = factor_of * jnp.repeat(jnp.exp(heights), extent[axis_at] // parts).reshape((-1,) + (1,) * (len(extent) - 1 - axis_at))
    return factor_of


def assign_block(rng, own, number, rows, amount, top, bound, lean):
    order = jax.random.permutation(rng, amount)
    packed, usual = shares(amount, rows * top, bound, lean, True), shares(amount, rows * top, bound, lean, False)
    places = jnp.arange(amount)

    def named(tallies, turn):
        used = int((tallies > 0).sum())
        fixed = max(1, used // 4)
        moved = fixed + (places - fixed + turn * (used - fixed)) % max(1, amount - fixed)
        return jnp.zeros((amount,), jnp.int32).at[order[jnp.where(places < fixed, places, moved)]].set(jnp.asarray(tallies, jnp.int32))

    tallies = jnp.where(number % 4 == 0, named(packed, number // 4), named(usual, number - number // 4 - 1))
    mixed = jax.random.permutation(jax.random.fold_in(own, 3), amount)
    giver, receiver = mixed[0:amount // 2 * 2:2], mixed[1:amount // 2 * 2:2]
    slack = jnp.minimum(tallies[giver] - 1, bound - tallies[receiver]) // 2
    slack = jnp.where((giver == order[0]) | (receiver == order[0]) | (tallies[receiver] == 0), 0, jnp.maximum(slack, 0))
    moved = jax.random.randint(jax.random.fold_in(own, 4), (amount // 2,), 0, 1 << 20) % (slack + 1)
    tallies = tallies.at[giver].add(-moved).at[receiver].add(moved)
    labels = jnp.searchsorted(jnp.cumsum(tallies), jnp.arange(rows * top), side="right").astype(jnp.int32)
    table = labels.reshape(top, rows).T
    table = table[jax.random.permutation(jax.random.fold_in(own, 1), rows)]
    turn = jax.random.randint(jax.random.fold_in(own, 2), (rows, 1), 0, top)
    return jnp.take_along_axis(table, (jnp.arange(top)[None, :] + turn) % top, axis=1)


def shares(amount, total, bound, slope, full):
    loads = [(1 << 20) // math.isqrt(grade ** slope) + 1 for grade in range(1, amount + 1)]
    largest = bound if full else min(bound, max(-(-total // amount), total * loads[0] // sum(loads)))
    least = 1 if total - largest >= amount - 1 else 0
    holding, spare = [largest] + [least] * (amount - 1), total - largest - least * (amount - 1)
    while spare > 0:
        candidates = [i for i in range(1, amount) if holding[i] < largest] or [i for i in range(1, amount) if holding[i] < bound]
        pool, left = sum([loads[i] for i in candidates]), spare
        for i in candidates:
            extra = min(bound - holding[i], max(1, left * loads[i] // pool), spare)
            holding[i] = holding[i] + extra
            spare = spare - extra
    return np.array(holding)


def bell_draw(stream_key, dims, width, reach, pieces=(), kind=jnp.bfloat16):
    entries = jax.random.normal(stream_key, dims, jnp.float32) * width
    if len(pieces) > 0:
        entries = levels(stream_key, dims, pieces, -0.22, 0.18) * entries
    return jnp.clip(entries, min=-reach, max=reach).astype(kind)


def setup_inputs(seed: int = 0) -> dict:
    keys = jax.random.split(jax.random.key(seed), 13)
    image_tokens = bell_draw(keys[0], (TOKENS, D), 1.0, 6.0, ((0, 8),))
    image_count = draw_image_count(jax.random.fold_in(keys[12], 71), 0)
    expert_routes_keys = jax.random.split(jax.random.fold_in(keys[2], 1), TOKENS // TOK_DEV)
    expert_routes_turns = jax.random.permutation(jax.random.fold_in(keys[2], 3), TOKENS // TOK_DEV)
    expert_routes = jax.vmap(lambda own, number: assign_block(jax.random.fold_in(keys[2], 2), own, number, TOK_DEV, EXPERTS, 2, CAP, 1))(expert_routes_keys, expert_routes_turns).reshape((TOKENS, 2))
    out_cotangent = bell_draw(keys[3], (TOKENS, D), 1.0, 6.0, ((0, 8),))
    norm_gains = jnp.clip(1.0 + 0.1 * jax.random.normal(keys[4], (LAYERS, 2, D), jnp.float32), 0.5, 1.5)
    attn_qkv = bell_draw(keys[5], (LAYERS, 3, D, D), D ** -0.5, 0.21875, ((3, 4),))
    attn_proj = bell_draw(keys[6], (LAYERS, D, D), (2 * D // SEQ) ** -0.5, 2.0, ((1, 4),))
    dense_up = bell_draw(keys[7], (D, FF), D ** -0.5, 0.21875, ((1, 4),))
    dense_down = bell_draw(keys[8], (FF, D), FF ** -0.5, 0.109375, ((0, 4),))
    router_weight = bell_draw(keys[9], (D, EXPERTS), (2 * D) ** -0.5, 0.15625, (), jnp.float32)
    expert_up = bell_draw(keys[10], (EXPERTS, D, FF), D ** -0.5, 0.21875, ((0, 8), (2, 4)))
    expert_down = bell_draw(keys[11], (EXPERTS, FF, D), (max(4 * FF // (9 * EXPERTS * EXPERTS), 1)) ** -0.5, 1.25, ((0, 8), (1, 4)))
    return {"image_tokens": image_tokens, "image_count": image_count, "expert_routes": expert_routes, "out_cotangent": out_cotangent, "norm_gains": norm_gains, "attn_qkv": attn_qkv, "attn_proj": attn_proj, "dense_up": dense_up, "dense_down": dense_down, "router_weight": router_weight, "expert_up": expert_up, "expert_down": expert_down}


@jax.custom_vjp
def low(v):
    return lax.optimization_barrier(v.astype(jnp.bfloat16)).astype(jnp.float32)

@jax.custom_vjp
def low_back(v):
    return v

def low_keep(v):
    return (low(v), None)

def low_pass(kept, grad):
    return (grad,)

def back_keep(v):
    return (v, None)

def back_low(kept, grad):
    return (low(grad),)
low.defvjp(low_keep, low_pass)
low_back.defvjp(back_keep, back_low)
highest = lax.Precision.HIGHEST
epsilon = 1e-06

def layer_norm(values, norm_gain):
    centered = values - lax.optimization_barrier(jnp.mean(values, axis=-1, keepdims=True))
    variance = lax.optimization_barrier(jnp.mean(centered * centered, axis=-1, keepdims=True))
    return centered * lax.rsqrt(variance + epsilon) * norm_gain

def place_slots(routes, counts):
    rows_all = jnp.arange(TOKENS, dtype=jnp.int32)
    live_rows = rows_all % TOK_DEV // SEQ < counts[rows_all // TOK_DEV]
    pairs = routes.reshape(N_DP, TOK_DEV * 2)
    live_pairs = jnp.repeat(live_rows, 2).reshape(N_DP, TOK_DEV * 2)
    onehot = ((pairs[..., None] == jnp.arange(EXPERTS, dtype=jnp.int32)) & live_pairs[..., None]).astype(jnp.int32)
    position = (jnp.cumsum(onehot, axis=1) - onehot).astype(jnp.int32)
    slot_rank = lax.optimization_barrier(jnp.sum(position * onehot, axis=-1)).astype(jnp.int32)
    source = jnp.arange(N_DP, dtype=jnp.int32)[:, None]
    slot_index = (pairs * N_DP + source) * CAP + slot_rank
    slot_index = jnp.where(live_pairs, slot_index, EXPERTS * N_DP * CAP).astype(jnp.int32)
    return (slot_index.reshape(TOKENS, 2), live_rows)

def attend_group(queries, key_rows, value_rows):
    scores = jnp.einsum('ishd,ithd->ihst', queries, key_rows, precision=highest) * HD ** (-0.5)
    scores = low_back(scores)
    weights = low(jax.nn.softmax(scores, axis=-1))
    return jnp.einsum('ihst,ithd->ishd', weights, value_rows, precision=highest)

def attend_packed(group):
    return attend_group(group[0], group[1], group[2])

def attention_branch(stream, norm_gain, qkv_weight, proj_weight):
    normed = low(layer_norm(stream, norm_gain))
    projected = jnp.einsum('td,jdc->jtc', normed, qkv_weight, precision=highest)
    projected = low(low_back(projected))
    grouped = projected.reshape(3, N_DP, IMG_SLOTS, SEQ, HEADS, HD)
    mixed = lax.map(jax.checkpoint(attend_packed), (grouped[0], grouped[1], grouped[2]))
    context = low(low_back(mixed.reshape(TOKENS, D)))
    return low_back(jnp.dot(context, proj_weight, precision=highest))

def dense_branch(stream, norm_gain, up_weight, down_weight):
    normed = low(layer_norm(stream, norm_gain))
    hidden = low_back(jnp.dot(normed, up_weight, precision=highest))
    hidden = low(jax.nn.gelu(hidden))
    return low_back(jnp.dot(hidden, down_weight, precision=highest))

def expert_branch(stream, norm_gain, router_w, up_weight, down_weight, slot_index, live_rows, routes):
    normed = low(layer_norm(stream, norm_gain))
    logits = jnp.dot(normed, router_w, precision=highest)
    gate_probs = jax.nn.softmax(logits, axis=-1)
    chosen = (routes[..., None] == jnp.arange(EXPERTS, dtype=jnp.int32)).astype(jnp.float32)
    gate_values = lax.optimization_barrier(jnp.sum(chosen * gate_probs[:, None, :], axis=-1)) * live_rows[:, None].astype(jnp.float32)
    flat_index = slot_index.reshape(-1)
    rows_in = jnp.zeros((EXPERTS * N_DP * CAP + 1, D), jnp.float32).at[flat_index].add(jnp.repeat(normed, 2, axis=0))
    rows_in = low_back(rows_in[:-1]).reshape(EXPERTS, N_DP * CAP, D)
    hidden = low_back(jnp.einsum('erd,edf->erf', rows_in, up_weight, precision=highest))
    hidden = low(jax.nn.gelu(hidden))
    rows_out = low(low_back(jnp.einsum('erf,efd->erd', hidden, down_weight, precision=highest)))
    padded = jnp.concatenate([rows_out.reshape(EXPERTS * N_DP * CAP, D), jnp.zeros((1, D), jnp.float32)], axis=0)
    picked = padded[slot_index]
    return lax.optimization_barrier(jnp.sum(gate_values[..., None] * picked, axis=1))

def reference(image_tokens, image_count, expert_routes, out_cotangent, norm_gains, attn_qkv, attn_proj, dense_up, dense_down, router_weight, expert_up, expert_down):
    slot_index, live_rows = place_slots(expert_routes, image_count)

    def forward(stream, gains, qkv_weight, proj_weight, up_weight, down_weight, router_w, ex_up, ex_down):
        stream = stream + attention_branch(stream, gains[0, 0], qkv_weight[0], proj_weight[0])
        stream = stream + dense_branch(stream, gains[0, 1], up_weight, down_weight)
        stream = stream + attention_branch(stream, gains[1, 0], qkv_weight[1], proj_weight[1])
        stream = stream + expert_branch(stream, gains[1, 1], router_w, ex_up, ex_down, slot_index, live_rows, expert_routes)
        return stream
    floats = (image_tokens.astype(jnp.float32), norm_gains.astype(jnp.float32), attn_qkv.astype(jnp.float32), attn_proj.astype(jnp.float32), dense_up.astype(jnp.float32), dense_down.astype(jnp.float32), router_weight.astype(jnp.float32), expert_up.astype(jnp.float32), expert_down.astype(jnp.float32))
    result, pullback = jax.vjp(forward, *floats)
    grads = pullback(out_cotangent.astype(jnp.float32))
    return (result.astype(jnp.bfloat16), grads[0], grads[1], grads[2], grads[3], grads[4], grads[5], grads[6], grads[7], grads[8])
```

```python
import jax
import jax.numpy as jnp
from jax import lax
from jax.sharding import PartitionSpec as P

HD = 64
SEQ = 197
PAD = 200

epsilon = 1e-06
highest = lax.Precision.HIGHEST
bf16 = jnp.bfloat16
f32 = jnp.float32


def matmul(left_side, right_side):
    return jnp.dot(left_side, right_side, preferred_element_type=f32)


def matmul_tn(left_side, right_side):
    return lax.dot_general(
        left_side, right_side, (((0,), (0,)), ((), ())), preferred_element_type=f32
    )


def matmul_nt(left_side, right_side):
    return lax.dot_general(
        left_side, right_side, (((1,), (1,)), ((), ())), preferred_element_type=f32
    )


def flip(values, mask):
    ranks = lax.axis_size("tensor")
    return lax.ppermute(values, "tensor", [(i, i ^ mask) for i in range(ranks)])


def after(values, earlier):
    return lax.optimization_barrier((values, earlier))[0]


def far(own, earlier=None):
    if earlier is not None:
        own = after(own, earlier)
    return flip(own, 2)


def near(own, far_own):
    return [own, flip(own, 1), far_own, flip(far_own, 1)]


def gather(own):
    return near(own, far(own))


def add_rounded(left_side, right_side):
    return (left_side.astype(f32) + right_side.astype(f32)).astype(bf16)


def scatter_sum(parts):
    mine = add_rounded(parts[0], flip(parts[1], 1))
    other = add_rounded(parts[2], flip(parts[3], 1))
    return add_rounded(mine, flip(other, 2))


def norm_forward(values, norm_gain):
    centered = values - jnp.mean(values, axis=-1, keepdims=True)
    inverse = lax.rsqrt(jnp.mean(centered * centered, axis=-1, keepdims=True) + epsilon)
    unit_rows = centered * inverse
    return (unit_rows * norm_gain, unit_rows, inverse)


def norm_backward(grad_out, norm_gain, unit_rows, inverse):
    grad_unit = grad_out * norm_gain
    grad_in = inverse * (
        grad_unit
        - jnp.mean(grad_unit, axis=-1, keepdims=True)
        - unit_rows * jnp.mean(grad_unit * unit_rows, axis=-1, keepdims=True)
    )
    return (grad_in, jnp.sum(grad_out * unit_rows, axis=0))


def masked_scores(queries, key_rows):
    scores = jnp.einsum(
        "ishd,ithd->ihst", queries, key_rows, preferred_element_type=f32
    ) * HD ** (-0.5)
    return jnp.where(jnp.arange(PAD) < SEQ, scores, -1e30)


def attention_forward(stream, norm_gain, qkv_w, proj_w):
    normed, unit_rows, inverse = norm_forward(stream, norm_gain)
    normed_b = normed.astype(bf16)
    tokens = normed_b.shape[0]
    projected = jnp.einsum("td,jcd->jtc", normed_b, qkv_w, preferred_element_type=f32)
    rounded = projected.astype(bf16).reshape(3, tokens // PAD, PAD, -1, HD)
    queries, key_rows, value_rows = (rounded[0], rounded[1], rounded[2])
    scores = masked_scores(queries, key_rows)
    row_peak = jnp.max(scores, axis=-1, keepdims=True)
    weights = jnp.exp(scores - row_peak)
    row_total = jnp.sum(weights, axis=-1, keepdims=True)
    log_total = row_peak + jnp.log(row_total)
    weights_b = (weights / row_total).astype(bf16)
    context = jnp.einsum("ihst,ithd->ishd", weights_b, value_rows, preferred_element_type=f32)
    context = context.astype(bf16).reshape(tokens, -1)
    return (
        stream + matmul(context, proj_w),
        (unit_rows, inverse, normed_b, queries, key_rows, value_rows, log_total, context),
    )


def attention_backward(grad_stream, norm_gain, qkv_w, proj_w, saved_state):
    unit_rows, inverse, normed_b, queries, key_rows, value_rows, log_total, context = saved_state
    tokens = normed_b.shape[0]
    grad_branch = grad_stream.astype(bf16)
    grad_proj = matmul_tn(context, grad_branch)
    grad_context = matmul_nt(grad_branch, proj_w).astype(bf16).reshape(queries.shape)
    probs_again = jnp.exp(masked_scores(queries, key_rows) - log_total)
    grad_weights = jnp.einsum(
        "ishd,ithd->ihst", grad_context, value_rows, preferred_element_type=f32
    )
    grad_values = jnp.einsum(
        "ihst,ishd->ithd", probs_again.astype(bf16), grad_context, preferred_element_type=f32
    )
    grad_scores = probs_again * (
        grad_weights - jnp.sum(probs_again * grad_weights, axis=-1, keepdims=True)
    )
    grad_scores = grad_scores.astype(bf16)
    grad_queries = jnp.einsum(
        "ihst,ithd->ishd", grad_scores, key_rows, preferred_element_type=f32
    ) * HD ** (-0.5)
    grad_keys = jnp.einsum(
        "ihst,ishd->ithd", grad_scores, queries, preferred_element_type=f32
    ) * HD ** (-0.5)
    stacked = (
        jnp.stack([grad_queries, grad_keys, grad_values]).astype(bf16).reshape(3, tokens, -1)
    )
    grad_qkv = jnp.einsum("jtc,td->jcd", stacked, normed_b, preferred_element_type=f32)
    grad_normed = jnp.einsum("jtc,jcd->td", stacked, qkv_w, preferred_element_type=f32)
    grad_in, grad_gain = norm_backward(grad_normed, norm_gain, unit_rows, inverse)
    return (grad_stream + grad_in, grad_qkv.astype(bf16), grad_proj.astype(bf16), grad_gain)


def dense_forward(stream, norm_gain, up_w, down_w):
    normed, unit_rows, inverse = norm_forward(stream, norm_gain)
    normed_b = normed.astype(bf16)
    hidden_pre = matmul(normed_b, up_w)
    hidden_b = jax.nn.gelu(hidden_pre).astype(bf16)
    return (
        stream + matmul(hidden_b, down_w),
        (unit_rows, inverse, normed_b, hidden_pre, hidden_b),
    )


def dense_backward(grad_stream, norm_gain, up_w, down_w, saved_state):
    unit_rows, inverse, normed_b, hidden_pre, hidden_b = saved_state
    grad_branch = grad_stream.astype(bf16)
    grad_down = matmul_tn(hidden_b, grad_branch)
    unused_out, gelu_back = jax.vjp(jax.nn.gelu, hidden_pre)
    grad_pre = gelu_back(matmul_nt(grad_branch, down_w))[0].astype(bf16)
    grad_up = matmul_tn(normed_b, grad_pre)
    grad_normed = matmul_nt(grad_pre, up_w)
    grad_in, grad_gain = norm_backward(grad_normed, norm_gain, unit_rows, inverse)
    return (grad_stream + grad_in, grad_up.astype(bf16), grad_down.astype(bf16), grad_gain)


def row_parts(values, axis):
    return jnp.split(values, lax.axis_size("tensor"), axis=axis)


def to_padded(rows):
    images = rows.shape[0] // SEQ
    padded = jnp.pad(rows.reshape(images, SEQ, -1), ((0, 0), (0, PAD - SEQ), (0, 0)))
    return padded.reshape(images * PAD, -1)


def in_order(blocks, me):
    ordered = [lax.select_n(me ^ a, *blocks) for a in range(len(blocks))]
    rows = jnp.stack(ordered).reshape(-1, PAD, blocks[0].shape[1])[:, :SEQ]
    return rows.reshape(-1, blocks[0].shape[1])


def all_to_all(rows):
    sources = lax.axis_size("dp")
    split_rows = rows.reshape(sources, -1, rows.shape[1])
    arrived = lax.all_to_all(split_rows, "dp", split_axis=0, concat_axis=0, tiled=True)
    return arrived.reshape(rows.shape)


def slots_of(routes, live_count):
    tokens = routes.shape[0]
    experts = lax.axis_size("dp")
    live_rows = jnp.arange(tokens, dtype=jnp.int32) // SEQ < live_count[0]
    chosen = routes[..., None] == jnp.arange(experts, dtype=jnp.int32)
    kept = (chosen & live_rows[:, None, None]).astype(jnp.int32).reshape(tokens * 2, experts)
    rank = jnp.sum((jnp.cumsum(kept, axis=0) - kept) * kept, axis=-1).reshape(tokens, 2)
    return jnp.where(live_rows[:, None], rank, -1)


def on_device(
    image_tokens,
    image_count,
    expert_routes,
    out_cotangent,
    norm_gains,
    attn_qkv,
    attn_proj,
    dense_up,
    dense_down,
    router_weight,
    expert_up,
    expert_down,
):
    ranks = lax.axis_size("tensor")
    experts = lax.axis_size("dp")
    me = lax.axis_index("tensor")
    tokens, width = image_tokens.shape
    own_rows = tokens // ranks
    block = own_rows // SEQ * PAD
    order = [me ^ k for k in range(ranks)]

    def own_of(whole):
        return lax.dynamic_slice_in_dim(whole, me * own_rows, own_rows, 0)

    qkv_t = jnp.swapaxes(attn_qkv, 2, 3)
    far_qkv0 = far(qkv_t[0])
    far_proj0 = far(attn_proj[0], far_qkv0)
    far_up = far(dense_up, far_proj0)
    far_down = far(dense_down, far_up)
    far_qkv1 = far(qkv_t[1], far_down)
    far_proj1 = far(attn_proj[1], far_qkv1)
    qkv0 = jnp.concatenate(near(qkv_t[0], far_qkv0), axis=1)
    proj0 = jnp.concatenate(near(attn_proj[0], far_proj0), axis=0)
    up_w = jnp.concatenate(near(dense_up, far_up), axis=1)
    down_w = jnp.concatenate(near(dense_down, far_down), axis=0)
    qkv1 = jnp.concatenate(near(qkv_t[1], far_qkv1), axis=1)
    proj1 = jnp.concatenate(near(attn_proj[1], far_proj1), axis=0)

    capacity = (2 * tokens + experts - 1) // experts + 2
    quota = -(-capacity // ranks)
    room = -(-quota // 8) * 8
    slots = experts * room
    rank = slots_of(expert_routes, image_count)
    holder = jnp.where(rank < 0, -1, rank // quota)
    place = expert_routes * room + rank - holder * quota
    mine = jnp.where(holder == me, place, -1)

    def blocked(values):
        images = tokens // SEQ
        padded = jnp.pad(
            values.T.reshape(2, images, SEQ), ((0, 0), (0, 0), (0, PAD - SEQ)), constant_values=-1
        ).reshape(2, ranks, block)
        return jnp.stack([padded[:, one] for one in order], axis=1)

    place_rel = blocked(mine).reshape(2, ranks * block)
    slot_ids = jnp.arange(slots, dtype=jnp.int32)[:, None]
    first = slot_ids == place_rel[0]
    second = slot_ids == place_rel[1]
    pick = (first | second).astype(bf16)
    pick_whole = ((slot_ids == mine[:, 0]) | (slot_ids == mine[:, 1])).astype(bf16)

    stream0 = to_padded(own_of(image_tokens)).astype(f32)
    grad_out = to_padded(own_of(out_cotangent)).astype(f32)
    stream1, attn0_state = attention_forward(stream0, norm_gains[0, 0], qkv0, proj0)
    stream2, dense_state = dense_forward(stream1, norm_gains[0, 1], up_w, down_w)
    stream3, attn1_state = attention_forward(stream2, norm_gains[1, 0], qkv1, proj1)

    normed, unit_rows, inverse = norm_forward(stream3, norm_gains[1, 1])
    normed_b = normed.astype(bf16)
    far_normed = far(normed_b, far_proj1)
    normed_all = jnp.concatenate(near(normed_b, far_normed), axis=0)
    far_ex_up = far(expert_up[0], far_normed)
    far_ex_down = far(expert_down[0], far_ex_up)
    ex_up = jnp.concatenate(near(expert_up[0], far_ex_up), axis=1)
    ex_down = jnp.concatenate(near(expert_down[0], far_ex_down), axis=0)

    rows_in = all_to_all(matmul(pick, normed_all).astype(bf16))
    logits = jnp.dot(normed_all.astype(f32), router_weight, precision=highest)
    gate_all = jax.nn.softmax(logits, axis=-1)
    gate_probs = gate_all[:block]
    routes_rel = blocked(expert_routes).reshape(2, ranks * block)
    expert_ids = jnp.arange(experts, dtype=jnp.int32)
    chosen_rel = routes_rel[..., None] == expert_ids
    gates = jnp.sum(jnp.where(chosen_rel, gate_all[None], 0.0), axis=-1)
    gate_slot = jnp.sum(
        jnp.where(first, gates[0], 0.0) + jnp.where(second, gates[1], 0.0), axis=1
    )[:, None]
    cot_slot = matmul(pick_whole, out_cotangent)
    grad_rows = all_to_all((gate_slot * cot_slot).astype(bf16))

    hidden_pre = matmul(rows_in, ex_up)
    hidden_b = jax.nn.gelu(hidden_pre).astype(bf16)
    rows_out = all_to_all(matmul(hidden_b, ex_down).astype(bf16))
    unused_out, gelu_back = jax.vjp(jax.nn.gelu, hidden_pre)
    grad_pre = gelu_back(matmul_nt(grad_rows, ex_down))[0].astype(bf16)
    grad_back = all_to_all(matmul_nt(grad_pre, ex_up).astype(bf16))
    grad_ex_down = scatter_sum(row_parts(matmul_tn(hidden_b, grad_rows).astype(bf16), 0))
    grad_ex_up = scatter_sum(row_parts(matmul_tn(rows_in, grad_pre).astype(bf16), 1))

    out_f = rows_out.astype(f32)
    gate_grad_slot = jnp.sum(cot_slot * out_f, axis=1)
    branch = matmul_tn(pick, (gate_slot * out_f).astype(bf16)).astype(bf16)
    stream4 = stream3 + scatter_sum(row_parts(branch, 0)).astype(f32)
    block_output = in_order(gather(stream4.astype(bf16)), me)

    own_holder = blocked(holder)[:, 0]
    own_place = blocked(place)[:, 0]
    own_routes = blocked(expert_routes)[:, 0]
    grad_gates = 0.0
    for one, values in zip(order, gather(gate_grad_slot)):
        here = jnp.where(own_holder == one, own_place, -1)
        found = here[..., None] == jnp.arange(slots, dtype=jnp.int32)
        grad_gates = grad_gates + jnp.sum(jnp.where(found, values, 0.0), axis=-1)
    grad_probs = jnp.sum(
        jnp.where(own_routes[..., None] == expert_ids, grad_gates[..., None], 0.0), axis=0
    )
    grad_logits = gate_probs * (
        grad_probs - jnp.sum(gate_probs * grad_probs, axis=-1, keepdims=True)
    )
    grad_router = jnp.dot(normed_b.astype(f32).T, grad_logits, precision=highest)
    grad_branch = matmul_tn(pick, grad_back).astype(bf16)
    grad_normed = scatter_sum(row_parts(grad_branch, 0)).astype(f32)
    grad_normed = grad_normed + jnp.dot(grad_logits, router_weight.T, precision=highest)
    grad_in, gain_expert = norm_backward(grad_normed, norm_gains[1, 1], unit_rows, inverse)
    grad3 = grad_out + grad_in

    def small_sum(values):
        values = values.astype(bf16)
        values = add_rounded(values, flip(values, 1))
        return add_rounded(values, flip(values, 2))

    def total(*parts):
        return lax.psum(jnp.concatenate(parts, axis=0), "dp").astype(f32)

    def qkv_rows(grad_qkv):
        own = scatter_sum(row_parts(grad_qkv, 1))
        return own.reshape(-1, width)

    grad2, grad_qkv1, grad_proj1, gain_attn1 = attention_backward(
        grad3, norm_gains[1, 0], qkv1, proj1, attn1_state
    )
    smalls1 = small_sum(
        jnp.concatenate([gain_attn1[None], gain_expert[None], grad_router.T], axis=0)
    )
    sums1 = total(qkv_rows(grad_qkv1), scatter_sum(row_parts(grad_proj1, 0)), smalls1)
    grad1, grad_up, grad_down, gain_dense = dense_backward(
        grad2, norm_gains[0, 1], up_w, down_w, dense_state
    )
    down_part = scatter_sum(row_parts(grad_down, 0))
    up_part = scatter_sum(row_parts(grad_up, 1))
    sums_dense = total(after(up_part, sums1), down_part)
    grad0, grad_qkv0, grad_proj0, gain_attn0 = attention_backward(
        grad1, norm_gains[0, 0], qkv0, proj0, attn0_state
    )
    smalls0 = small_sum(jnp.concatenate([gain_attn0[None], gain_dense[None]], axis=0))
    proj_part0 = scatter_sum(row_parts(grad_proj0, 0))
    sums0 = total(after(qkv_rows(grad_qkv0), sums_dense), proj_part0, smalls0)
    input_grad = in_order(gather(grad0.astype(bf16)), me).astype(f32)

    columns = attn_qkv.shape[3]
    grad_qkv = jnp.stack(
        [jnp.swapaxes(sums[: 3 * columns].reshape(3, columns, width), 1, 2) for sums in (sums0, sums1)]
    )
    grad_proj = jnp.stack([sums[3 * columns : 4 * columns] for sums in (sums0, sums1)])
    grad_gains = jnp.stack(
        [sums[4 * columns : 4 * columns + 2] for sums in (sums0, sums1)]
    )
    router_grad = sums1[4 * columns + 2 :].T
    return (
        block_output,
        input_grad,
        grad_gains,
        grad_qkv,
        grad_proj,
        sums_dense[:width],
        sums_dense[width:],
        router_grad,
        grad_ex_up.astype(f32)[None],
        grad_ex_down.astype(f32)[None],
    )


def solution(mesh):
    return jax.shard_map(
        on_device,
        mesh=mesh,
        in_specs=(
            P("dp", None),
            P("dp"),
            P("dp", None),
            P("dp", None),
            P(),
            P(None, None, None, "tensor"),
            P(None, "tensor", None),
            P(None, "tensor"),
            P("tensor", None),
            P(),
            P("dp", None, "tensor"),
            P("dp", "tensor", None),
        ),
        out_specs=(
            P("dp", None),
            P("dp", None),
            P(),
            P(None, None, None, "tensor"),
            P(None, "tensor", None),
            P(None, "tensor"),
            P("tensor", None),
            P(),
            P("dp", None, "tensor"),
            P("dp", "tensor", None),
        ),
        check_vma=False,
    )
```

```python
import jax
import jax.numpy as jnp
from jax import lax
from jax.experimental import pallas as pl
from jax.experimental.pallas import tpu as pltpu
from jax.sharding import PartitionSpec as P

HD = 64
SEQ = 197
PAD = 208

epsilon = 1e-06
highest = lax.Precision.HIGHEST
bf16 = jnp.bfloat16
f32 = jnp.float32


def matmul(left_side, right_side):
    return jnp.dot(left_side, right_side, preferred_element_type=f32)


def matmul_tn(left_side, right_side):
    return lax.dot_general(
        left_side, right_side, (((0,), (0,)), ((), ())), preferred_element_type=f32
    )


def matmul_nt(left_side, right_side):
    return lax.dot_general(
        left_side, right_side, (((1,), (1,)), ((), ())), preferred_element_type=f32
    )


def flip(values, mask):
    ranks = lax.axis_size("tensor")
    return lax.ppermute(values, "tensor", [(i, i ^ mask) for i in range(ranks)])


def after(values, earlier):
    return lax.optimization_barrier((values, earlier))[0]


def far(own, earlier=None):
    if earlier is not None:
        own = after(own, earlier)
    return flip(own, 2)


def near(own, far_own):
    return [own, flip(own, 1), far_own, flip(far_own, 1)]


def gather(own):
    return near(own, far(own))


def add_rounded(left_side, right_side):
    return (left_side.astype(f32) + right_side.astype(f32)).astype(bf16)


def near_sum(parts):
    mine = add_rounded(parts[0], flip(parts[1], 1))
    other = add_rounded(parts[2], flip(parts[3], 1))
    return (mine, other)


def far_sum(pair, earlier=None):
    mine, other = pair
    return add_rounded(mine, far(other, earlier))


def dp_flip(values, bit):
    groups = lax.axis_size("dp")
    return lax.ppermute(values, "dp", [(i, i ^ (1 << bit)) for i in range(groups)])


def dp_bits():
    return list(range(lax.axis_size("dp").bit_length() - 1))


def upper(bit):
    return (lax.axis_index("dp") >> bit) % 2 == 1


def dp_halve(values, bit):
    half = values.shape[0] // 2
    low, high = values[:half], values[half:]
    kept = jnp.where(upper(bit), high, low)
    sent = jnp.where(upper(bit), low, high)
    return add_rounded(kept, dp_flip(sent, bit))


def dp_double(values, bit):
    arrived = dp_flip(values, bit)
    return jnp.concatenate(
        [jnp.where(upper(bit), arrived, values), jnp.where(upper(bit), values, arrived)], axis=0
    )


def dp_halves(values, bits):
    for bit in bits:
        values = dp_halve(values, bit)
    return values


def dp_doubles(values, bits):
    for bit in reversed(bits):
        values = dp_double(values, bit)
    return values


def dp_rows(*parts):
    rows = jnp.concatenate(parts, axis=0)
    unit = 8 * lax.axis_size("dp")
    return jnp.pad(rows, ((0, -rows.shape[0] % unit), (0, 0)))


def norm_forward(values, norm_gain):
    centered = values - jnp.mean(values, axis=-1, keepdims=True)
    inverse = lax.rsqrt(jnp.mean(centered * centered, axis=-1, keepdims=True) + epsilon)
    unit_rows = centered * inverse
    return (unit_rows * norm_gain, unit_rows, inverse)


def norm_backward(grad_out, norm_gain, unit_rows, inverse):
    grad_unit = grad_out * norm_gain
    grad_in = inverse * (
        grad_unit
        - jnp.mean(grad_unit, axis=-1, keepdims=True)
        - unit_rows * jnp.mean(grad_unit * unit_rows, axis=-1, keepdims=True)
    )
    return (grad_in, jnp.sum(grad_out * unit_rows, axis=0))


def half_masks():
    lane = lax.broadcasted_iota(jnp.int32, (1, 2 * HD), 1)
    return [(lane // HD == one).astype(f32).astype(bf16) for one in range(2)]


def head_probs(queries, key_rows):
    scores = matmul_nt(queries, key_rows) * HD ** (-0.5)
    column = lax.broadcasted_iota(jnp.int32, (1, PAD), 1)
    scores = jnp.where(column < SEQ, scores, -1e30)
    weights = jnp.exp(scores - jnp.max(scores, axis=-1, keepdims=True))
    return weights / jnp.sum(weights, axis=-1, keepdims=True)


def context_kernel(qkv_ref, context_ref):
    masks = half_masks()
    for first in range(0, context_ref.shape[1], 2 * HD):
        columns = slice(first, first + 2 * HD)
        queries, key_rows, value_rows = (qkv_ref[one, 0, :, columns] for one in range(3))
        total = 0.0
        for mask in masks:
            weights = head_probs(queries * mask, key_rows).astype(bf16)
            total = total + matmul(weights, value_rows * mask)
        context_ref[:, columns] = total.astype(bf16)


def context_grad_kernel(qkv_ref, grad_ref, out_ref):
    masks = half_masks()
    scale = HD ** (-0.5)
    for first in range(0, grad_ref.shape[1], 2 * HD):
        columns = slice(first, first + 2 * HD)
        queries, key_rows, value_rows = (qkv_ref[one, 0, :, columns] for one in range(3))
        grad_context = grad_ref[:, columns]
        grad_queries, grad_keys, grad_values = 0.0, 0.0, 0.0
        for mask in masks:
            own_queries, own_grad = queries * mask, grad_context * mask
            probs = head_probs(own_queries, key_rows)
            grad_weights = matmul_nt(own_grad, value_rows)
            grad_values = grad_values + matmul_tn(probs.astype(bf16), own_grad)
            grad_scores = probs * (
                grad_weights - jnp.sum(probs * grad_weights, axis=-1, keepdims=True)
            )
            grad_scores = grad_scores.astype(bf16)
            grad_queries = grad_queries + matmul(grad_scores, key_rows * mask)
            grad_keys = grad_keys + matmul_tn(grad_scores, own_queries)
        out_ref[0, 0, :, columns] = (grad_queries * scale).astype(bf16)
        out_ref[1, 0, :, columns] = (grad_keys * scale).astype(bf16)
        out_ref[2, 0, :, columns] = grad_values.astype(bf16)


def attend(qkv):
    images, width = qkv.shape[1], qkv.shape[3]
    return pl.pallas_call(
        context_kernel,
        grid=(images,),
        in_specs=[pl.BlockSpec((3, 1, PAD, width), lambda i: (0, i, 0, 0))],
        out_specs=pl.BlockSpec((PAD, width), lambda i: (i, 0)),
        out_shape=jax.ShapeDtypeStruct((images * PAD, width), bf16),
        compiler_params=pltpu.CompilerParams(vmem_limit_bytes=32 * 1024 * 1024),
        cost_estimate=pl.CostEstimate(
            flops=4 * images * PAD * PAD * width,
            bytes_accessed=8 * images * PAD * width,
            transcendentals=images * PAD * PAD * width // HD,
        ),
    )(qkv)


def attend_grad(qkv, grad_context):
    images, width = qkv.shape[1], qkv.shape[3]
    return pl.pallas_call(
        context_grad_kernel,
        grid=(images,),
        in_specs=[
            pl.BlockSpec((3, 1, PAD, width), lambda i: (0, i, 0, 0)),
            pl.BlockSpec((PAD, width), lambda i: (i, 0)),
        ],
        out_specs=pl.BlockSpec((3, 1, PAD, width), lambda i: (0, i, 0, 0)),
        out_shape=jax.ShapeDtypeStruct(qkv.shape, bf16),
        compiler_params=pltpu.CompilerParams(vmem_limit_bytes=32 * 1024 * 1024),
        cost_estimate=pl.CostEstimate(
            flops=10 * images * PAD * PAD * width,
            bytes_accessed=14 * images * PAD * width,
            transcendentals=images * PAD * PAD * width // HD,
        ),
    )(qkv, grad_context)


def attention_forward(stream, norm_gain, qkv_w, proj_w):
    normed, unit_rows, inverse = norm_forward(stream, norm_gain)
    normed_b = normed.astype(bf16)
    projected = jnp.einsum("td,jcd->jtc", normed_b, qkv_w, preferred_element_type=f32)
    qkv = projected.astype(bf16).reshape(3, -1, PAD, qkv_w.shape[1])
    context = attend(qkv)
    return (stream + matmul(context, proj_w), (unit_rows, inverse, normed_b, qkv, context))


def attention_backward(grad_stream, norm_gain, qkv_w, proj_w, saved_state, between=None):
    unit_rows, inverse, normed_b, qkv, context = saved_state
    tokens = normed_b.shape[0]
    grad_branch = grad_stream.astype(bf16)
    grad_proj = matmul_tn(context, grad_branch)
    grad_context = matmul_nt(grad_branch, proj_w).astype(bf16)
    stacked = attend_grad(qkv, grad_context).reshape(3, tokens, -1)
    if between is not None:
        stacked = between(stacked)
    grad_qkv = jnp.einsum("jtc,td->jcd", stacked, normed_b, preferred_element_type=f32)
    grad_normed = jnp.einsum("jtc,jcd->td", stacked, qkv_w, preferred_element_type=f32)
    grad_in, grad_gain = norm_backward(grad_normed, norm_gain, unit_rows, inverse)
    return (grad_stream + grad_in, grad_qkv.astype(bf16), grad_proj.astype(bf16), grad_gain)


def dense_forward(stream, norm_gain, up_w, down_w):
    normed, unit_rows, inverse = norm_forward(stream, norm_gain)
    normed_b = normed.astype(bf16)
    hidden_pre = matmul(normed_b, up_w)
    hidden_b = jax.nn.gelu(hidden_pre).astype(bf16)
    return (
        stream + matmul(hidden_b, down_w),
        (unit_rows, inverse, normed_b, hidden_pre, hidden_b),
    )


def dense_backward(grad_stream, norm_gain, up_w, down_w, saved_state):
    unit_rows, inverse, normed_b, hidden_pre, hidden_b = saved_state
    grad_branch = grad_stream.astype(bf16)
    grad_down = matmul_tn(hidden_b, grad_branch)
    unused_out, gelu_back = jax.vjp(jax.nn.gelu, hidden_pre)
    grad_pre = gelu_back(matmul_nt(grad_branch, down_w))[0].astype(bf16)
    grad_up = matmul_tn(normed_b, grad_pre)
    grad_normed = matmul_nt(grad_pre, up_w)
    grad_in, grad_gain = norm_backward(grad_normed, norm_gain, unit_rows, inverse)
    return (grad_stream + grad_in, grad_up.astype(bf16), grad_down.astype(bf16), grad_gain)


def row_parts(values, axis):
    return jnp.split(values, lax.axis_size("tensor"), axis=axis)


def to_padded(rows):
    images = rows.shape[0] // SEQ
    padded = jnp.pad(rows.reshape(images, SEQ, -1), ((0, 0), (0, PAD - SEQ), (0, 0)))
    return padded.reshape(images * PAD, -1)


def in_order(blocks, me):
    ordered = [lax.select_n(me ^ a, *blocks) for a in range(len(blocks))]
    rows = jnp.stack(ordered).reshape(-1, PAD, blocks[0].shape[1])[:, :SEQ]
    return rows.reshape(-1, blocks[0].shape[1])


def all_to_all(rows):
    sources = lax.axis_size("dp")
    split_rows = rows.reshape(sources, -1, rows.shape[1])
    arrived = lax.all_to_all(split_rows, "dp", split_axis=0, concat_axis=0, tiled=True)
    return arrived.reshape(rows.shape)


def slots_of(routes, live_count):
    tokens = routes.shape[0]
    experts = lax.axis_size("dp")
    live_rows = jnp.arange(tokens, dtype=jnp.int32) // SEQ < live_count[0]
    chosen = routes[..., None] == jnp.arange(experts, dtype=jnp.int32)
    kept = (chosen & live_rows[:, None, None]).astype(jnp.int32).reshape(tokens * 2, experts)
    rank = jnp.sum((jnp.cumsum(kept, axis=0) - kept) * kept, axis=-1).reshape(tokens, 2)
    return jnp.where(live_rows[:, None], rank, -1)


def on_device(
    image_tokens,
    image_count,
    expert_routes,
    out_cotangent,
    norm_gains,
    attn_qkv,
    attn_proj,
    dense_up,
    dense_down,
    router_weight,
    expert_up,
    expert_down,
):
    ranks = lax.axis_size("tensor")
    experts = lax.axis_size("dp")
    me = lax.axis_index("tensor")
    tokens, width = image_tokens.shape
    own_rows = tokens // ranks
    block = own_rows // SEQ * PAD
    order = [me ^ k for k in range(ranks)]

    def own_of(whole):
        return lax.dynamic_slice_in_dim(whole, me * own_rows, own_rows, 0)

    qkv_t = jnp.swapaxes(attn_qkv, 2, 3)
    far_qkv0 = far(qkv_t[0])
    far_proj0 = far(attn_proj[0], far_qkv0)
    far_up = far(dense_up, far_proj0)
    far_down = far(dense_down, far_up)
    far_qkv1 = far(qkv_t[1], far_down)
    far_proj1 = far(attn_proj[1], far_qkv1)
    far_ex_up = far(expert_up[0], far_proj1)
    qkv0 = jnp.concatenate(near(qkv_t[0], far_qkv0), axis=1)
    proj0 = jnp.concatenate(near(attn_proj[0], far_proj0), axis=0)
    up_w = jnp.concatenate(near(dense_up, far_up), axis=1)
    down_w = jnp.concatenate(near(dense_down, far_down), axis=0)
    qkv1 = jnp.concatenate(near(qkv_t[1], far_qkv1), axis=1)
    proj1 = jnp.concatenate(near(attn_proj[1], far_proj1), axis=0)

    capacity = (2 * tokens + experts - 1) // experts + 2
    quota = -(-capacity // ranks)
    room = -(-quota // 8) * 8
    slots = experts * room
    rank = slots_of(expert_routes, image_count)
    holder = jnp.where(rank < 0, -1, rank // quota)
    place = expert_routes * room + rank - holder * quota
    mine = jnp.where(holder == me, place, -1)

    def blocked(values):
        images = tokens // SEQ
        padded = jnp.pad(
            values.T.reshape(2, images, SEQ), ((0, 0), (0, 0), (0, PAD - SEQ)), constant_values=-1
        ).reshape(2, ranks, block)
        return jnp.stack([padded[:, one] for one in order], axis=1)

    place_rel = blocked(mine).reshape(2, ranks * block)
    slot_ids = jnp.arange(slots, dtype=jnp.int32)[:, None]
    first = slot_ids == place_rel[0]
    second = slot_ids == place_rel[1]
    pick = (first | second).astype(bf16)
    pick_whole = ((slot_ids == mine[:, 0]) | (slot_ids == mine[:, 1])).astype(bf16)

    stream0 = to_padded(own_of(image_tokens)).astype(f32)
    grad_out = to_padded(own_of(out_cotangent)).astype(f32)
    stream1, attn0_state = attention_forward(stream0, norm_gains[0, 0], qkv0, proj0)
    stream2, dense_state = dense_forward(stream1, norm_gains[0, 1], up_w, down_w)
    stream3, attn1_state = attention_forward(stream2, norm_gains[1, 0], qkv1, proj1)

    normed, unit_rows, inverse = norm_forward(stream3, norm_gains[1, 1])
    normed_b = normed.astype(bf16)
    far_normed = far(normed_b)
    normed_all = jnp.concatenate(near(normed_b, far_normed), axis=0)
    far_ex_down = far(expert_down[0], (far_normed, far_ex_up))
    ex_up = jnp.concatenate(near(expert_up[0], far_ex_up), axis=1)
    ex_down = jnp.concatenate(near(expert_down[0], far_ex_down), axis=0)

    rows_in = all_to_all(matmul(pick, normed_all).astype(bf16))
    logits = jnp.dot(normed_all.astype(f32), router_weight, precision=highest)
    gate_all = jax.nn.softmax(logits, axis=-1)
    gate_probs = gate_all[:block]
    routes_rel = blocked(expert_routes).reshape(2, ranks * block)
    expert_ids = jnp.arange(experts, dtype=jnp.int32)
    chosen_rel = routes_rel[..., None] == expert_ids
    gates = jnp.sum(jnp.where(chosen_rel, gate_all[None], 0.0), axis=-1)
    gate_slot = jnp.sum(
        jnp.where(first, gates[0], 0.0) + jnp.where(second, gates[1], 0.0), axis=1
    )[:, None]
    cot_slot = matmul(pick_whole, out_cotangent)
    grad_rows = all_to_all((gate_slot * cot_slot).astype(bf16))

    hidden_pre = matmul(rows_in, ex_up)
    hidden_b = jax.nn.gelu(hidden_pre).astype(bf16)
    rows_out = all_to_all(matmul(hidden_b, ex_down).astype(bf16))
    unused_out, gelu_back = jax.vjp(jax.nn.gelu, hidden_pre)
    grad_pre = gelu_back(matmul_nt(grad_rows, ex_down))[0].astype(bf16)
    grad_back = all_to_all(matmul_nt(grad_pre, ex_up).astype(bf16))
    down_pair = near_sum(row_parts(matmul_tn(hidden_b, grad_rows).astype(bf16), 0))
    grad_ex_down = far_sum(down_pair)
    up_pair = near_sum(row_parts(matmul_tn(rows_in, grad_pre).astype(bf16), 1))
    grad_back, up_pair, grad_ex_down = lax.optimization_barrier((grad_back, up_pair, grad_ex_down))

    out_f = rows_out.astype(f32)
    gate_grad_slot = jnp.sum(cot_slot * out_f, axis=1)
    branch = matmul_tn(pick, (gate_slot * out_f).astype(bf16)).astype(bf16)

    own_holder = blocked(holder)[:, 0]
    own_place = blocked(place)[:, 0]
    own_routes = blocked(expert_routes)[:, 0]
    grad_gates = 0.0
    for one, values in zip(order, gather(gate_grad_slot)):
        here = jnp.where(own_holder == one, own_place, -1)
        found = here[..., None] == jnp.arange(slots, dtype=jnp.int32)
        grad_gates = grad_gates + jnp.sum(jnp.where(found, values, 0.0), axis=-1)
    grad_probs = jnp.sum(
        jnp.where(own_routes[..., None] == expert_ids, grad_gates[..., None], 0.0), axis=0
    )
    grad_logits = gate_probs * (
        grad_probs - jnp.sum(gate_probs * grad_probs, axis=-1, keepdims=True)
    )
    grad_router = jnp.dot(normed_b.astype(f32).T, grad_logits, precision=highest)
    grad_branch = matmul_tn(pick, grad_back).astype(bf16)
    grad_normed = far_sum(near_sum(row_parts(grad_branch, 0)))
    grad_ex_up = far_sum(up_pair, grad_normed)
    grad_normed = grad_normed.astype(f32) + jnp.dot(grad_logits, router_weight.T, precision=highest)
    grad_in, gain_expert = norm_backward(grad_normed, norm_gains[1, 1], unit_rows, inverse)
    grad3 = grad_out + grad_in

    def small_sum(values):
        values = values.astype(bf16)
        values = add_rounded(values, flip(values, 1))
        return add_rounded(values, flip(values, 2))

    columns = attn_qkv.shape[3]
    bits = dp_bits()

    def attn_pair(grad_qkv, grad_proj):
        pairs = [near_sum(row_parts(grad_qkv, 1)), near_sum(row_parts(grad_proj, 0))]
        return tuple(
            jnp.concatenate([qkv_part.reshape(-1, width), proj_part], axis=0)
            for qkv_part, proj_part in zip(*pairs)
        )

    grad2, grad_qkv1, grad_proj1, gain_attn1 = attention_backward(
        grad3, norm_gains[1, 0], qkv1, proj1, attn1_state
    )
    attn1_pair = attn_pair(grad_qkv1, grad_proj1)
    smalls1 = small_sum(
        jnp.concatenate([gain_attn1[None], gain_expert[None], grad_router.T], axis=0)
    )
    grad2, attn1_pair, grad_ex_up = lax.optimization_barrier((grad2, attn1_pair, grad_ex_up))
    attn1_sum = far_sum(attn1_pair)
    grad1, grad_up, grad_down, gain_dense = dense_backward(
        grad2, norm_gains[0, 1], up_w, down_w, dense_state
    )
    down_pair = near_sum(row_parts(grad_down, 0))
    up_pair = near_sum(row_parts(grad_up, 1))
    grad1, down_pair, up_pair, attn1_sum, smalls1 = lax.optimization_barrier(
        (grad1, down_pair, up_pair, attn1_sum, smalls1)
    )
    attn1_part = dp_halve(dp_rows(attn1_sum, smalls1), bits[0])
    down_sum = far_sum(down_pair)

    def between(values):
        nonlocal attn1_part, down_sum
        values, attn1_part, down_sum = lax.optimization_barrier((values, attn1_part, down_sum))
        return values

    grad0, grad_qkv0, grad_proj0, gain_attn0 = attention_backward(
        grad1, norm_gains[0, 0], qkv0, proj0, attn0_state, between
    )
    attn1_part = dp_halves(attn1_part, bits[1:])
    down_part = dp_halve(dp_rows(down_sum), bits[0])
    attn0_pair = attn_pair(grad_qkv0, grad_proj0)
    smalls0 = small_sum(jnp.concatenate([gain_attn0[None], gain_dense[None]], axis=0))
    up_sum = far_sum(up_pair, down_sum)
    attn0_sum = far_sum(attn0_pair, up_sum)
    down_part = dp_halves(down_part, bits[1:])
    up_part = dp_halves(dp_rows(up_sum), bits)
    attn0_part = dp_halves(dp_rows(attn0_sum, smalls0), bits)
    sums1 = dp_doubles(attn1_part, bits).astype(f32)
    sums_down = dp_doubles(down_part, bits).astype(f32)
    sums_up = dp_doubles(up_part, bits).astype(f32)
    sums0 = dp_doubles(attn0_part, bits).astype(f32)

    grad0_b = grad0.astype(bf16)
    far_grad0 = far(grad0_b, attn0_sum)
    input_grad = in_order(near(grad0_b, far_grad0), me).astype(f32)
    branch_sum = far_sum(near_sum(row_parts(branch, 0)), far_grad0)
    stream4 = (stream3 + branch_sum.astype(f32)).astype(bf16)
    block_output = in_order(near(stream4, far(stream4)), me)

    grad_qkv = jnp.stack(
        [
            jnp.swapaxes(sums[: 3 * columns].reshape(3, columns, width), 1, 2)
            for sums in (sums0, sums1)
        ]
    )
    grad_proj = jnp.stack([sums[3 * columns : 4 * columns] for sums in (sums0, sums1)])
    grad_gains = jnp.stack([sums[4 * columns : 4 * columns + 2] for sums in (sums0, sums1)])
    router_grad = sums1[4 * columns + 2 : 4 * columns + 2 + experts].T
    return (
        block_output,
        input_grad,
        grad_gains,
        grad_qkv,
        grad_proj,
        sums_up,
        sums_down,
        router_grad,
        grad_ex_up.astype(f32)[None],
        grad_ex_down.astype(f32)[None],
    )


def solution(mesh):
    return jax.shard_map(
        on_device,
        mesh=mesh,
        in_specs=(
            P("dp", None),
            P("dp"),
            P("dp", None),
            P("dp", None),
            P(),
            P(None, None, None, "tensor"),
            P(None, "tensor", None),
            P(None, "tensor"),
            P("tensor", None),
            P(),
            P("dp", None, "tensor"),
            P("dp", "tensor", None),
        ),
        out_specs=(
            P("dp", None),
            P("dp", None),
            P(),
            P(None, None, None, "tensor"),
            P(None, "tensor", None),
            P(None, "tensor"),
            P("tensor", None),
            P(),
            P("dp", None, "tensor"),
            P("dp", "tensor", None),
        ),
        check_vma=False,
    )
```

```python
import jax
import jax.numpy as jnp
from jax import lax
from jax.experimental import pallas as pl
from jax.experimental.pallas import tpu as pltpu
from jax.sharding import PartitionSpec as P

HD = 64
SEQ = 197
PAD = 208

epsilon = 1e-06
highest = lax.Precision.HIGHEST
bf16 = jnp.bfloat16
f32 = jnp.float32


def matmul(left_side, right_side):
    return jnp.dot(left_side, right_side, preferred_element_type=f32)


def matmul_tn(left_side, right_side):
    return lax.dot_general(
        left_side, right_side, (((0,), (0,)), ((), ())), preferred_element_type=f32
    )


def matmul_nt(left_side, right_side):
    return lax.dot_general(
        left_side, right_side, (((1,), (1,)), ((), ())), preferred_element_type=f32
    )


def flip(values, mask):
    ranks = lax.axis_size("tensor")
    return lax.ppermute(values, "tensor", [(i, i ^ mask) for i in range(ranks)])


def after(values, earlier):
    return lax.optimization_barrier((values, earlier))[0]


def far(own, earlier=None):
    if earlier is not None:
        own = after(own, earlier)
    return flip(own, 2)


def near(own, far_own):
    return [own, flip(own, 1), far_own, flip(far_own, 1)]


def gather(own):
    return near(own, far(own))


def add_rounded(left_side, right_side):
    return (left_side.astype(f32) + right_side.astype(f32)).astype(bf16)


def near_sum(parts):
    mine = add_rounded(parts[0], flip(parts[1], 1))
    other = add_rounded(parts[2], flip(parts[3], 1))
    return (mine, other)


def far_sum(pair, earlier=None):
    mine, other = pair
    return add_rounded(mine, far(other, earlier))


def dp_flip(values, bit):
    groups = lax.axis_size("dp")
    return lax.ppermute(values, "dp", [(i, i ^ (1 << bit)) for i in range(groups)])


def dp_bits():
    return list(range(lax.axis_size("dp").bit_length() - 1))


def upper(bit):
    return (lax.axis_index("dp") >> bit) % 2 == 1


def dp_halve(values, bit):
    half = values.shape[0] // 2
    low, high = values[:half], values[half:]
    kept = jnp.where(upper(bit), high, low)
    sent = jnp.where(upper(bit), low, high)
    return add_rounded(kept, dp_flip(sent, bit))


def dp_double(values, bit):
    arrived = dp_flip(values, bit)
    return jnp.concatenate(
        [jnp.where(upper(bit), arrived, values), jnp.where(upper(bit), values, arrived)], axis=0
    )


def dp_halves(values, bits):
    for bit in bits:
        values = dp_halve(values, bit)
    return values


def dp_doubles(values, bits):
    for bit in reversed(bits):
        values = dp_double(values, bit)
    return values


def dp_rows(*parts):
    rows = jnp.concatenate(parts, axis=0)
    unit = 16 * lax.axis_size("dp")
    return jnp.pad(rows, ((0, -rows.shape[0] % unit), (0, 0)))


def join(*values):
    return lax.optimization_barrier(values)


def norm_forward(values, norm_gain):
    centered = values - jnp.mean(values, axis=-1, keepdims=True)
    inverse = lax.rsqrt(jnp.mean(centered * centered, axis=-1, keepdims=True) + epsilon)
    unit_rows = centered * inverse
    return (unit_rows * norm_gain, unit_rows, inverse)


def norm_backward(grad_out, norm_gain, unit_rows, inverse):
    grad_unit = grad_out * norm_gain
    grad_in = inverse * (
        grad_unit
        - jnp.mean(grad_unit, axis=-1, keepdims=True)
        - unit_rows * jnp.mean(grad_unit * unit_rows, axis=-1, keepdims=True)
    )
    return (grad_in, jnp.sum(grad_out * unit_rows, axis=0))


def half_masks():
    lane = lax.broadcasted_iota(jnp.int32, (1, 2 * HD), 1)
    return [(lane // HD == one).astype(f32).astype(bf16) for one in range(2)]


def head_probs(queries, key_rows):
    scores = matmul_nt(queries, key_rows) * HD ** (-0.5)
    column = lax.broadcasted_iota(jnp.int32, (1, PAD), 1)
    scores = jnp.where(column < SEQ, scores, -1e30)
    weights = jnp.exp(scores - jnp.max(scores, axis=-1, keepdims=True))
    return weights / jnp.sum(weights, axis=-1, keepdims=True)


def context_kernel(qkv_ref, context_ref):
    masks = half_masks()
    for first in range(0, context_ref.shape[1], 2 * HD):
        columns = slice(first, first + 2 * HD)
        queries, key_rows, value_rows = (qkv_ref[one, 0, :, columns] for one in range(3))
        total = 0.0
        for mask in masks:
            weights = head_probs(queries * mask, key_rows).astype(bf16)
            total = total + matmul(weights, value_rows * mask)
        context_ref[:, columns] = total.astype(bf16)


def context_grad_kernel(qkv_ref, grad_ref, out_ref):
    masks = half_masks()
    scale = HD ** (-0.5)
    for first in range(0, grad_ref.shape[1], 2 * HD):
        columns = slice(first, first + 2 * HD)
        queries, key_rows, value_rows = (qkv_ref[one, 0, :, columns] for one in range(3))
        grad_context = grad_ref[:, columns]
        grad_queries, grad_keys, grad_values = 0.0, 0.0, 0.0
        for mask in masks:
            own_queries, own_grad = queries * mask, grad_context * mask
            probs = head_probs(own_queries, key_rows)
            grad_weights = matmul_nt(own_grad, value_rows)
            grad_values = grad_values + matmul_tn(probs.astype(bf16), own_grad)
            grad_scores = probs * (
                grad_weights - jnp.sum(probs * grad_weights, axis=-1, keepdims=True)
            )
            grad_scores = grad_scores.astype(bf16)
            grad_queries = grad_queries + matmul(grad_scores, key_rows * mask)
            grad_keys = grad_keys + matmul_tn(grad_scores, own_queries)
        out_ref[0, 0, :, columns] = (grad_queries * scale).astype(bf16)
        out_ref[1, 0, :, columns] = (grad_keys * scale).astype(bf16)
        out_ref[2, 0, :, columns] = grad_values.astype(bf16)


def attend(qkv):
    images, width = qkv.shape[1], qkv.shape[3]
    return pl.pallas_call(
        context_kernel,
        grid=(images,),
        in_specs=[pl.BlockSpec((3, 1, PAD, width), lambda i: (0, i, 0, 0))],
        out_specs=pl.BlockSpec((PAD, width), lambda i: (i, 0)),
        out_shape=jax.ShapeDtypeStruct((images * PAD, width), bf16),
        compiler_params=pltpu.CompilerParams(vmem_limit_bytes=32 * 1024 * 1024),
        cost_estimate=pl.CostEstimate(
            flops=4 * images * PAD * PAD * width,
            bytes_accessed=8 * images * PAD * width,
            transcendentals=images * PAD * PAD * width // HD,
        ),
    )(qkv)


def attend_grad(qkv, grad_context):
    images, width = qkv.shape[1], qkv.shape[3]
    return pl.pallas_call(
        context_grad_kernel,
        grid=(images,),
        in_specs=[
            pl.BlockSpec((3, 1, PAD, width), lambda i: (0, i, 0, 0)),
            pl.BlockSpec((PAD, width), lambda i: (i, 0)),
        ],
        out_specs=pl.BlockSpec((3, 1, PAD, width), lambda i: (0, i, 0, 0)),
        out_shape=jax.ShapeDtypeStruct(qkv.shape, bf16),
        compiler_params=pltpu.CompilerParams(vmem_limit_bytes=32 * 1024 * 1024),
        cost_estimate=pl.CostEstimate(
            flops=10 * images * PAD * PAD * width,
            bytes_accessed=14 * images * PAD * width,
            transcendentals=images * PAD * PAD * width // HD,
        ),
    )(qkv, grad_context)


def attention_forward(stream, norm_gain, qkv_w, proj_w):
    normed, unit_rows, inverse = norm_forward(stream, norm_gain)
    normed_b = normed.astype(bf16)
    projected = jnp.einsum("td,jcd->jtc", normed_b, qkv_w, preferred_element_type=f32)
    qkv = projected.astype(bf16).reshape(3, -1, PAD, qkv_w.shape[1])
    context = attend(qkv)
    return (stream + matmul(context, proj_w), (unit_rows, inverse, normed_b, qkv, context))


def attention_backward(grad_stream, norm_gain, qkv_w, proj_w, saved_state, between=None):
    unit_rows, inverse, normed_b, qkv, context = saved_state
    tokens = normed_b.shape[0]
    grad_branch = grad_stream.astype(bf16)
    grad_proj = matmul_tn(context, grad_branch)
    grad_context = matmul_nt(grad_branch, proj_w).astype(bf16)
    stacked = attend_grad(qkv, grad_context).reshape(3, tokens, -1)
    if between is not None:
        stacked = between(stacked)
    grad_qkv = jnp.einsum("jtc,td->jcd", stacked, normed_b, preferred_element_type=f32)
    grad_normed = jnp.einsum("jtc,jcd->td", stacked, qkv_w, preferred_element_type=f32)
    grad_in, grad_gain = norm_backward(grad_normed, norm_gain, unit_rows, inverse)
    return (grad_stream + grad_in, grad_qkv.astype(bf16), grad_proj.astype(bf16), grad_gain)


def row_parts(values, axis):
    return jnp.split(values, lax.axis_size("tensor"), axis=axis)


def to_padded(rows):
    images = rows.shape[0] // SEQ
    padded = jnp.pad(rows.reshape(images, SEQ, -1), ((0, 0), (0, PAD - SEQ), (0, 0)))
    return padded.reshape(images * PAD, -1)


def in_order(blocks, me):
    ordered = [lax.select_n(me ^ a, *blocks) for a in range(len(blocks))]
    rows = jnp.stack(ordered).reshape(-1, PAD, blocks[0].shape[1])[:, :SEQ]
    return rows.reshape(-1, blocks[0].shape[1])


def all_to_all(rows):
    sources = lax.axis_size("dp")
    split_rows = rows.reshape(sources, -1, rows.shape[1])
    arrived = lax.all_to_all(split_rows, "dp", split_axis=0, concat_axis=0, tiled=True)
    return arrived.reshape(rows.shape)


def slots_of(routes, live_count):
    tokens = routes.shape[0]
    experts = lax.axis_size("dp")
    live_rows = jnp.arange(tokens, dtype=jnp.int32) // SEQ < live_count[0]
    chosen = routes[..., None] == jnp.arange(experts, dtype=jnp.int32)
    kept = (chosen & live_rows[:, None, None]).astype(jnp.int32).reshape(tokens * 2, experts)
    rank = jnp.sum((jnp.cumsum(kept, axis=0) - kept) * kept, axis=-1).reshape(tokens, 2)
    return jnp.where(live_rows[:, None], rank, -1)


def on_device(
    image_tokens,
    image_count,
    expert_routes,
    out_cotangent,
    norm_gains,
    attn_qkv,
    attn_proj,
    dense_up,
    dense_down,
    router_weight,
    expert_up,
    expert_down,
):
    ranks = lax.axis_size("tensor")
    experts = lax.axis_size("dp")
    me = lax.axis_index("tensor")
    tokens, width = image_tokens.shape
    own_rows = tokens // ranks
    block = own_rows // SEQ * PAD
    order = [me ^ k for k in range(ranks)]

    def own_of(whole):
        return lax.dynamic_slice_in_dim(whole, me * own_rows, own_rows, 0)

    bits = dp_bits()
    qkv_t = jnp.swapaxes(attn_qkv, 2, 3)
    columns = qkv_t.shape[2]
    far_qkv0 = far(qkv_t[0])
    far_proj0 = far(attn_proj[0], far_qkv0)
    far_qkv1 = far(qkv_t[1], far_qkv0)
    qkv0 = jnp.concatenate(near(qkv_t[0], far_qkv0), axis=1)
    far_proj0 = after(far_proj0, qkv0)
    proj0 = jnp.concatenate(near(attn_proj[0], far_proj0), axis=0)

    capacity = (2 * tokens + experts - 1) // experts + 2
    quota = -(-capacity // ranks)
    room = -(-(quota + 3) // 8) * 8
    slots = experts * room
    rank = slots_of(expert_routes, image_count)
    holder = jnp.where(rank < 0, -1, rank // quota)
    place = expert_routes * room + rank - holder * quota
    mine = jnp.where(holder == me, place, -1)

    def blocked(values):
        images = tokens // SEQ
        padded = jnp.pad(
            values.T.reshape(2, images, SEQ), ((0, 0), (0, 0), (0, PAD - SEQ)), constant_values=-1
        ).reshape(2, ranks, block)
        return jnp.stack([padded[:, one] for one in order], axis=1)

    place_rel = blocked(mine).reshape(2, ranks * block)
    slot_ids = jnp.arange(slots, dtype=jnp.int32)[:, None]
    first = slot_ids == place_rel[0]
    second = slot_ids == place_rel[1]
    pick = (first | second).astype(bf16)
    pick_whole = ((slot_ids == mine[:, 0]) | (slot_ids == mine[:, 1])).astype(bf16)

    stream0 = to_padded(own_of(image_tokens)).astype(f32)
    grad_out = to_padded(own_of(out_cotangent)).astype(f32)
    stream1, attn0_state = attention_forward(stream0, norm_gains[0, 0], qkv0, proj0)
    stream1, far_qkv1 = join(stream1, far_qkv1)

    normed_m, dense_unit, dense_inverse = norm_forward(stream1, norm_gains[0, 1])
    normed_m = normed_m.astype(bf16)
    far_normed_m = far(normed_m)
    cot_slot = matmul(pick_whole, out_cotangent)
    far_normed_m, cot_slot = join(far_normed_m, cot_slot)
    cot_in = all_to_all(cot_slot.astype(bf16))
    normed_m = jnp.concatenate(near(normed_m, far_normed_m), axis=0)
    dense_pre = matmul(normed_m, dense_up)
    dense_hidden = jax.nn.gelu(dense_pre).astype(bf16)
    dense_pair = near_sum(row_parts(matmul(dense_hidden, dense_down).astype(bf16), 0))
    dense_sum = far_sum(dense_pair)
    far_proj1 = far(attn_proj[1], dense_sum)
    half = expert_up.shape[1] // 2
    far_ex_up = far(expert_up[0, :half], far_proj1)
    stream2 = stream1 + dense_sum.astype(f32)
    qkv1 = jnp.concatenate(near(qkv_t[1], far_qkv1), axis=1)
    proj1 = jnp.concatenate(near(attn_proj[1], far_proj1), axis=0)
    stream3, attn1_state = attention_forward(stream2, norm_gains[1, 0], qkv1, proj1)

    stream3, cot_in, far_ex_up = join(stream3, cot_in, far_ex_up)
    normed, unit_rows, inverse = norm_forward(stream3, norm_gains[1, 1])
    normed_b = normed.astype(bf16)
    far_normed = far(normed_b)
    logits = jnp.dot(normed_b.astype(f32), router_weight, precision=highest)
    gate_probs = jax.nn.softmax(logits, axis=-1)
    gate_all = jnp.stack(gather(gate_probs.T))
    routes_rel = blocked(expert_routes)
    expert_ids = jnp.arange(experts, dtype=jnp.int32)
    gates = jnp.sum(
        jnp.where(routes_rel[:, :, None] == expert_ids[:, None], gate_all[None], 0.0), axis=2
    ).reshape(2, ranks * block)
    gate_slot = jnp.sum(
        jnp.where(first, gates[0], 0.0) + jnp.where(second, gates[1], 0.0), axis=1
    )
    parts, left = [], gate_slot
    for _ in range(3):
        parts.append(lax.optimization_barrier(left.astype(bf16)))
        left = left - parts[-1].astype(f32)
    far_ex_up_rest = far(expert_up[0, half:], far_normed)
    far_normed, gate_slot, parts = join(far_normed, gate_slot, parts)
    normed_all = jnp.concatenate(near(normed_b, far_normed), axis=0)
    far_ex_down = far(expert_down[0], far_ex_up_rest)
    far_ex_up = jnp.concatenate([far_ex_up, far_ex_up_rest], axis=0)
    send = matmul(pick, normed_all).astype(bf16).reshape(experts, room, width)
    row = jnp.arange(room, dtype=jnp.int32)[:, None]
    for at, part in enumerate(parts):
        lanes = jnp.pad(part.reshape(experts, 1, room), ((0, 0), (0, 0), (0, width - room)))
        send = jnp.where(row == quota + at, lanes, send)
    rows_in = all_to_all(send.reshape(slots, width))
    ex_up = jnp.concatenate(near(expert_up[0], far_ex_up), axis=1)
    rows_in, ex_up = join(rows_in, ex_up)
    ex_down = jnp.concatenate(near(expert_down[0], far_ex_down), axis=0)
    gate_rows = rows_in.reshape(experts, room, width)[:, quota : quota + 3, :room]
    gate_in = jnp.sum(gate_rows.astype(f32), axis=1).reshape(slots, 1)
    grad_rows = (gate_in * cot_in.astype(f32)).astype(bf16)

    hidden_pre = matmul(rows_in, ex_up)
    hidden_b = jax.nn.gelu(hidden_pre).astype(bf16)
    send_out = matmul(hidden_b, ex_down).astype(bf16)
    rows_out = all_to_all(send_out)
    unused_out, gelu_back = jax.vjp(jax.nn.gelu, hidden_pre)
    grad_pre = gelu_back(matmul_nt(grad_rows, ex_down))[0].astype(bf16)
    late_rows = after(grad_rows, send_out)
    down_pair = near_sum(row_parts(matmul_tn(hidden_b, late_rows).astype(bf16), 0))
    grad_pre, rows_out, down_pair = join(grad_pre, rows_out, down_pair)
    send_back = matmul_nt(grad_pre, ex_up).astype(bf16)
    grad_ex_down = far_sum(down_pair)
    send_back, grad_pre = join(send_back, grad_pre)
    grad_back = all_to_all(send_back)
    grad_pre, grad_ex_down = join(grad_pre, grad_ex_down)
    up_pair = near_sum(row_parts(matmul_tn(rows_in, grad_pre).astype(bf16), 1))

    out_f = rows_out.astype(f32)
    gate_grad_slot = jnp.sum(cot_slot * out_f, axis=1)
    branch = matmul_tn(pick, (gate_slot[:, None] * out_f).astype(bf16)).astype(bf16)

    own_holder = blocked(holder)[:, 0]
    own_place = blocked(place)[:, 0]
    own_routes = blocked(expert_routes)[:, 0]
    grad_gates = 0.0
    for one, values in zip(order, gather(gate_grad_slot)):
        here = jnp.where(own_holder == one, own_place, -1)
        found = here[..., None] == jnp.arange(slots, dtype=jnp.int32)
        grad_gates = grad_gates + jnp.sum(jnp.where(found, values, 0.0), axis=-1)
    grad_probs = jnp.sum(
        jnp.where(own_routes[..., None] == expert_ids, grad_gates[..., None], 0.0), axis=0
    )
    grad_logits = gate_probs * (
        grad_probs - jnp.sum(gate_probs * grad_probs, axis=-1, keepdims=True)
    )
    grad_router = jnp.dot(normed_b.astype(f32).T, grad_logits, precision=highest)
    grad_back, grad_logits, branch, ex_up_pair = join(grad_back, grad_logits, branch, up_pair)
    grad_branch = matmul_tn(pick, grad_back).astype(bf16)
    grad_normed = far_sum(near_sum(row_parts(grad_branch, 0)))
    grad_normed = grad_normed.astype(f32) + jnp.dot(grad_logits, router_weight.T, precision=highest)
    grad_in, gain_expert = norm_backward(grad_normed, norm_gains[1, 1], unit_rows, inverse)
    grad3 = grad_out + grad_in

    def small_sum(values):
        values = values.astype(bf16)
        values = add_rounded(values, flip(values, 1))
        return add_rounded(values, flip(values, 2))

    def own_pair(*grads):
        pairs = [near_sum(row_parts(one, axis)) for one, axis in grads]
        return tuple(
            jnp.concatenate([one.reshape(-1, width) for one in side], axis=0)
            for side in zip(*pairs)
        )

    order_a = bits
    order_b = [bits[1], bits[0]] + bits[2:]

    def halve_both(pair, step):
        return (dp_halve(pair[0], order_a[step]), dp_halve(pair[1], order_b[step]))

    def double_both(pair, step):
        return (dp_double(pair[0], order_a[step]), dp_double(pair[1], order_b[step]))

    last = len(bits) - 1
    grad2, grad_qkv1, grad_proj1, gain_attn1 = attention_backward(
        grad3, norm_gains[1, 0], qkv1, proj1, attn1_state
    )
    grad2_b = grad2.astype(bf16)
    far_grad2 = far(grad2_b)
    attn1_pair = own_pair((grad_qkv1, 1), (grad_proj1, 0))
    far_grad2, attn1_pair = join(far_grad2, attn1_pair)
    grad2_all = jnp.concatenate(near(grad2_b, far_grad2), axis=0)
    unused_out, gelu_back = jax.vjp(jax.nn.gelu, dense_pre)
    dense_grad = gelu_back(matmul_nt(grad2_all, dense_down))[0].astype(bf16)
    dense_grad_pair = near_sum(row_parts(matmul_nt(dense_grad, dense_up).astype(bf16), 0))
    branch_sum = far_sum(near_sum(row_parts(branch, 0)), far_grad2)
    dense_grad_pair, branch_sum = join(dense_grad_pair, branch_sum)
    grad_normed_m = far_sum(dense_grad_pair)
    attn1_sum = far_sum(attn1_pair, grad_normed_m)
    grad_up = matmul_tn(normed_m, dense_grad).astype(bf16)
    grad_down = matmul_tn(dense_hidden, grad2_all).astype(bf16)
    grad_normed_m, grad_up, grad_down = join(grad_normed_m, grad_up, grad_down)
    dense_parts = halve_both((dp_rows(grad_up), dp_rows(grad_down)), 0)
    grad_in, gain_dense = norm_backward(
        grad_normed_m.astype(f32), norm_gains[0, 1], dense_unit, dense_inverse
    )
    grad1 = grad2 + grad_in

    def between(values):
        nonlocal dense_parts
        values, dense_parts = join(values, dense_parts)
        dense_parts = halve_both(dense_parts, 1)
        return values

    grad0, grad_qkv0, grad_proj0, gain_attn0 = attention_backward(
        grad1, norm_gains[0, 0], qkv0, proj0, attn0_state, between
    )
    attn0_pair = own_pair((grad_qkv0, 1), (grad_proj0, 0))
    smalls = small_sum(
        jnp.concatenate(
            [gain_attn0[None], gain_dense[None], gain_attn1[None], gain_expert[None], grad_router.T],
            axis=0,
        )
    )
    grad0, dense_parts, attn1_sum, attn0_pair, smalls = join(
        grad0, dense_parts, attn1_sum, attn0_pair, smalls
    )
    attn0_sum = far_sum(attn0_pair)
    attn_sums = lax.psum(jnp.concatenate([attn0_sum, attn1_sum, smalls], axis=0), "dp")
    for step in range(2, last + 1):
        dense_parts = halve_both(dense_parts, step)
    for step in range(last, -1, -1):
        dense_parts = double_both(dense_parts, step)
    dense_up_sum = dense_parts[0][: dense_up.shape[0]].astype(f32)
    dense_down_sum = dense_parts[1][: dense_down.shape[0]].astype(f32)

    grad0_b = grad0.astype(bf16)
    far_grad0 = far(grad0_b, attn0_sum)
    stream4 = (stream3 + branch_sum.astype(f32)).astype(bf16)
    far_stream4 = far(stream4, far_grad0)
    grad_ex_up = far_sum(ex_up_pair, far_stream4)
    input_grad = in_order(near(grad0_b, far_grad0), me).astype(f32)
    block_output = in_order(near(stream4, far_stream4), me)
    attn_sums, block_output, input_grad, grad_ex_up, dense_up_sum, dense_down_sum = join(
        attn_sums, block_output, input_grad, grad_ex_up, dense_up_sum, dense_down_sum
    )
    attn_sums = attn_sums.astype(f32)
    sums0, sums1 = attn_sums[: 4 * columns], attn_sums[4 * columns : 8 * columns]

    grad_qkv = jnp.stack(
        [
            jnp.swapaxes(sums[: 3 * columns].reshape(3, columns, width), 1, 2)
            for sums in (sums0, sums1)
        ]
    )
    grad_proj = jnp.stack([sums[3 * columns : 4 * columns] for sums in (sums0, sums1)])
    smalls = attn_sums[8 * columns :]
    grad_gains = smalls[:4].reshape(2, 2, width)
    router_grad = smalls[4 : 4 + experts].T
    return (
        block_output,
        input_grad,
        grad_gains,
        grad_qkv,
        grad_proj,
        dense_up_sum,
        dense_down_sum,
        router_grad,
        grad_ex_up.astype(f32)[None],
        grad_ex_down.astype(f32)[None],
    )


def solution(mesh):
    return jax.shard_map(
        on_device,
        mesh=mesh,
        in_specs=(
            P("dp", None),
            P("dp"),
            P("dp", None),
            P("dp", None),
            P(),
            P(None, None, None, "tensor"),
            P(None, "tensor", None),
            P(None, "tensor"),
            P("tensor", None),
            P(),
            P("dp", None, "tensor"),
            P("dp", "tensor", None),
        ),
        out_specs=(
            P("dp", None),
            P("dp", None),
            P(),
            P(None, None, None, "tensor"),
            P(None, "tensor", None),
            P(None, "tensor"),
            P("tensor", None),
            P(),
            P("dp", None, "tensor"),
            P("dp", "tensor", None),
        ),
        check_vma=False,
    )
```

```python
import jax
import jax.numpy as jnp
from jax import lax
from jax.experimental import pallas as pl
from jax.experimental.pallas import tpu as pltpu
from jax.sharding import PartitionSpec as P

HD = 64
SEQ = 197
PAD = 208

epsilon = 1e-06
highest = lax.Precision.HIGHEST
bf16 = jnp.bfloat16
f32 = jnp.float32


def matmul(left_side, right_side):
    return jnp.dot(left_side, right_side, preferred_element_type=f32)


def matmul_tn(left_side, right_side):
    return lax.dot_general(
        left_side, right_side, (((0,), (0,)), ((), ())), preferred_element_type=f32
    )


def matmul_nt(left_side, right_side):
    return lax.dot_general(
        left_side, right_side, (((1,), (1,)), ((), ())), preferred_element_type=f32
    )


def flip(values, mask):
    ranks = lax.axis_size("tensor")
    return lax.ppermute(values, "tensor", [(i, i ^ mask) for i in range(ranks)])


def after(values, earlier):
    return lax.optimization_barrier((values, earlier))[0]


def far(own, earlier=None):
    if earlier is not None:
        own = after(own, earlier)
    return flip(own, 2)


def near(own, far_own):
    return [own, flip(own, 1), far_own, flip(far_own, 1)]


def gather(own):
    return near(own, far(own))


def add_rounded(left_side, right_side):
    return (left_side.astype(f32) + right_side.astype(f32)).astype(bf16)


def near_sum(parts):
    mine = add_rounded(parts[0], flip(parts[1], 1))
    other = add_rounded(parts[2], flip(parts[3], 1))
    return (mine, other)


def far_sum(pair, earlier=None):
    mine, other = pair
    return add_rounded(mine, far(other, earlier))


def dp_flip(values, bit):
    groups = lax.axis_size("dp")
    return lax.ppermute(values, "dp", [(i, i ^ (1 << bit)) for i in range(groups)])


def dp_bits():
    return list(range(lax.axis_size("dp").bit_length() - 1))


def upper(bit):
    return (lax.axis_index("dp") >> bit) % 2 == 1


def dp_halve(values, bit):
    half = values.shape[0] // 2
    low, high = values[:half], values[half:]
    kept = jnp.where(upper(bit), high, low)
    sent = jnp.where(upper(bit), low, high)
    return add_rounded(kept, dp_flip(sent, bit))


def dp_double(values, bit):
    arrived = dp_flip(values, bit)
    return jnp.concatenate(
        [jnp.where(upper(bit), arrived, values), jnp.where(upper(bit), values, arrived)], axis=0
    )


def dp_halves(values, bits):
    for bit in bits:
        values = dp_halve(values, bit)
    return values


def dp_doubles(values, bits):
    for bit in reversed(bits):
        values = dp_double(values, bit)
    return values


def dp_rows(*parts):
    rows = jnp.concatenate(parts, axis=0)
    unit = 16 * lax.axis_size("dp")
    return jnp.pad(rows, ((0, -rows.shape[0] % unit), (0, 0)))


def join(*values):
    return lax.optimization_barrier(values)


def norm_forward(values, norm_gain):
    centered = values - jnp.mean(values, axis=-1, keepdims=True)
    inverse = lax.rsqrt(jnp.mean(centered * centered, axis=-1, keepdims=True) + epsilon)
    unit_rows = centered * inverse
    return (unit_rows * norm_gain, unit_rows, inverse)


def norm_backward(grad_out, norm_gain, unit_rows, inverse):
    grad_unit = grad_out * norm_gain
    grad_in = inverse * (
        grad_unit
        - jnp.mean(grad_unit, axis=-1, keepdims=True)
        - unit_rows * jnp.mean(grad_unit * unit_rows, axis=-1, keepdims=True)
    )
    return (grad_in, jnp.sum(grad_out * unit_rows, axis=0))


def half_masks():
    lane = lax.broadcasted_iota(jnp.int32, (1, 2 * HD), 1)
    return [(lane // HD == one).astype(f32).astype(bf16) for one in range(2)]


def head_probs(queries, key_rows):
    scores = matmul_nt(queries, key_rows) * HD ** (-0.5)
    column = lax.broadcasted_iota(jnp.int32, (1, PAD), 1)
    scores = jnp.where(column < SEQ, scores, -1e30)
    weights = jnp.exp(scores - jnp.max(scores, axis=-1, keepdims=True))
    return weights / jnp.sum(weights, axis=-1, keepdims=True)


def context_kernel(qkv_ref, context_ref):
    masks = half_masks()
    for first in range(0, context_ref.shape[1], 2 * HD):
        columns = slice(first, first + 2 * HD)
        queries, key_rows, value_rows = (qkv_ref[one, 0, :, columns] for one in range(3))
        total = 0.0
        for mask in masks:
            weights = head_probs(queries * mask, key_rows).astype(bf16)
            total = total + matmul(weights, value_rows * mask)
        context_ref[:, columns] = total.astype(bf16)


def context_grad_kernel(qkv_ref, grad_ref, out_ref):
    masks = half_masks()
    scale = HD ** (-0.5)
    for first in range(0, grad_ref.shape[1], 2 * HD):
        columns = slice(first, first + 2 * HD)
        queries, key_rows, value_rows = (qkv_ref[one, 0, :, columns] for one in range(3))
        grad_context = grad_ref[:, columns]
        grad_queries, grad_keys, grad_values = 0.0, 0.0, 0.0
        for mask in masks:
            own_queries, own_grad = queries * mask, grad_context * mask
            probs = head_probs(own_queries, key_rows)
            grad_weights = matmul_nt(own_grad, value_rows)
            grad_values = grad_values + matmul_tn(probs.astype(bf16), own_grad)
            grad_scores = probs * (
                grad_weights - jnp.sum(probs * grad_weights, axis=-1, keepdims=True)
            )
            grad_scores = grad_scores.astype(bf16)
            grad_queries = grad_queries + matmul(grad_scores, key_rows * mask)
            grad_keys = grad_keys + matmul_tn(grad_scores, own_queries)
        out_ref[0, 0, :, columns] = (grad_queries * scale).astype(bf16)
        out_ref[1, 0, :, columns] = (grad_keys * scale).astype(bf16)
        out_ref[2, 0, :, columns] = grad_values.astype(bf16)


def attend(qkv):
    images, width = qkv.shape[1], qkv.shape[3]
    return pl.pallas_call(
        context_kernel,
        grid=(images,),
        in_specs=[pl.BlockSpec((3, 1, PAD, width), lambda i: (0, i, 0, 0))],
        out_specs=pl.BlockSpec((PAD, width), lambda i: (i, 0)),
        out_shape=jax.ShapeDtypeStruct((images * PAD, width), bf16),
        compiler_params=pltpu.CompilerParams(vmem_limit_bytes=32 * 1024 * 1024),
        cost_estimate=pl.CostEstimate(
            flops=4 * images * PAD * PAD * width,
            bytes_accessed=8 * images * PAD * width,
            transcendentals=images * PAD * PAD * width // HD,
        ),
    )(qkv)


def attend_grad(qkv, grad_context):
    images, width = qkv.shape[1], qkv.shape[3]
    return pl.pallas_call(
        context_grad_kernel,
        grid=(images,),
        in_specs=[
            pl.BlockSpec((3, 1, PAD, width), lambda i: (0, i, 0, 0)),
            pl.BlockSpec((PAD, width), lambda i: (i, 0)),
        ],
        out_specs=pl.BlockSpec((3, 1, PAD, width), lambda i: (0, i, 0, 0)),
        out_shape=jax.ShapeDtypeStruct(qkv.shape, bf16),
        compiler_params=pltpu.CompilerParams(vmem_limit_bytes=32 * 1024 * 1024),
        cost_estimate=pl.CostEstimate(
            flops=10 * images * PAD * PAD * width,
            bytes_accessed=14 * images * PAD * width,
            transcendentals=images * PAD * PAD * width // HD,
        ),
    )(qkv, grad_context)


def attention_forward(stream, norm_gain, qkv_w, proj_w):
    normed, unit_rows, inverse = norm_forward(stream, norm_gain)
    normed_b = normed.astype(bf16)
    projected = jnp.einsum("td,jcd->jtc", normed_b, qkv_w, preferred_element_type=f32)
    qkv = projected.astype(bf16).reshape(3, -1, PAD, qkv_w.shape[1])
    context = attend(qkv)
    return (stream + matmul(context, proj_w), (unit_rows, inverse, normed_b, qkv, context))


def attention_backward(grad_stream, norm_gain, qkv_w, proj_w, saved_state, between=None):
    unit_rows, inverse, normed_b, qkv, context = saved_state
    tokens = normed_b.shape[0]
    grad_branch = grad_stream.astype(bf16)
    grad_proj = matmul_tn(context, grad_branch)
    grad_context = matmul_nt(grad_branch, proj_w).astype(bf16)
    stacked = attend_grad(qkv, grad_context).reshape(3, tokens, -1)
    if between is not None:
        stacked = between(stacked)
    grad_qkv = jnp.einsum("jtc,td->jcd", stacked, normed_b, preferred_element_type=f32)
    grad_normed = jnp.einsum("jtc,jcd->td", stacked, qkv_w, preferred_element_type=f32)
    grad_in, grad_gain = norm_backward(grad_normed, norm_gain, unit_rows, inverse)
    return (grad_stream + grad_in, grad_qkv.astype(bf16), grad_proj.astype(bf16), grad_gain)


def row_parts(values, axis):
    return jnp.split(values, lax.axis_size("tensor"), axis=axis)


def to_padded(rows):
    images = rows.shape[0] // SEQ
    padded = jnp.pad(rows.reshape(images, SEQ, -1), ((0, 0), (0, PAD - SEQ), (0, 0)))
    return padded.reshape(images * PAD, -1)


def in_order(blocks, me):
    ordered = [lax.select_n(me ^ a, *blocks) for a in range(len(blocks))]
    rows = jnp.stack(ordered).reshape(-1, PAD, blocks[0].shape[1])[:, :SEQ]
    return rows.reshape(-1, blocks[0].shape[1])


def all_to_all(rows):
    sources = lax.axis_size("dp")
    split_rows = rows.reshape(sources, -1, rows.shape[1])
    arrived = lax.all_to_all(split_rows, "dp", split_axis=0, concat_axis=0, tiled=True)
    return arrived.reshape(rows.shape)


def slots_of(routes, live_count):
    tokens = routes.shape[0]
    experts = lax.axis_size("dp")
    live_rows = jnp.arange(tokens, dtype=jnp.int32) // SEQ < live_count[0]
    chosen = routes[..., None] == jnp.arange(experts, dtype=jnp.int32)
    kept = (chosen & live_rows[:, None, None]).astype(jnp.int32).reshape(tokens * 2, experts)
    rank = jnp.sum((jnp.cumsum(kept, axis=0) - kept) * kept, axis=-1).reshape(tokens, 2)
    return jnp.where(live_rows[:, None], rank, -1)


def on_device(
    image_tokens,
    image_count,
    expert_routes,
    out_cotangent,
    norm_gains,
    attn_qkv,
    attn_proj,
    dense_up,
    dense_down,
    router_weight,
    expert_up,
    expert_down,
):
    ranks = lax.axis_size("tensor")
    experts = lax.axis_size("dp")
    me = lax.axis_index("tensor")
    tokens, width = image_tokens.shape
    own_rows = tokens // ranks
    block = own_rows // SEQ * PAD
    order = [me ^ k for k in range(ranks)]

    def own_of(whole):
        return lax.dynamic_slice_in_dim(whole, me * own_rows, own_rows, 0)

    bits = dp_bits()
    qkv_t = jnp.swapaxes(attn_qkv, 2, 3)
    columns = qkv_t.shape[2]
    far_qkv0 = far(qkv_t[0])
    far_proj0 = far(attn_proj[0], far_qkv0)
    far_qkv1 = far(qkv_t[1], far_qkv0)
    qkv0 = jnp.concatenate(near(qkv_t[0], far_qkv0), axis=1)
    far_proj0 = after(far_proj0, qkv0)
    proj0 = jnp.concatenate(near(attn_proj[0], far_proj0), axis=0)

    capacity = (2 * tokens + experts - 1) // experts + 2
    quota = -(-capacity // ranks)
    room = -(-(quota + 3) // 8) * 8
    slots = experts * room
    rank = slots_of(expert_routes, image_count)
    holder = jnp.where(rank < 0, -1, rank // quota)
    place = expert_routes * room + rank - holder * quota
    mine = jnp.where(holder == me, place, -1)

    def blocked(values):
        images = tokens // SEQ
        padded = jnp.pad(
            values.T.reshape(2, images, SEQ), ((0, 0), (0, 0), (0, PAD - SEQ)), constant_values=-1
        ).reshape(2, ranks, block)
        return jnp.stack([padded[:, one] for one in order], axis=1)

    place_rel = blocked(mine).reshape(2, ranks * block)
    slot_ids = jnp.arange(slots, dtype=jnp.int32)[:, None]
    first = slot_ids == place_rel[0]
    second = slot_ids == place_rel[1]
    pick = (first | second).astype(bf16)
    pick_whole = ((slot_ids == mine[:, 0]) | (slot_ids == mine[:, 1])).astype(bf16)

    stream0 = to_padded(own_of(image_tokens)).astype(f32)
    grad_out = to_padded(own_of(out_cotangent)).astype(f32)
    stream1, attn0_state = attention_forward(stream0, norm_gains[0, 0], qkv0, proj0)
    stream1, far_qkv1 = join(stream1, far_qkv1)

    normed_m, dense_unit, dense_inverse = norm_forward(stream1, norm_gains[0, 1])
    normed_m = normed_m.astype(bf16)
    far_normed_m = far(normed_m)
    cot_slot = matmul(pick_whole, out_cotangent)
    far_normed_m, cot_slot = join(far_normed_m, cot_slot)
    cot_in = all_to_all(cot_slot.astype(bf16))
    normed_m = jnp.concatenate(near(normed_m, far_normed_m), axis=0)
    dense_pre = matmul(normed_m, dense_up)
    dense_hidden = jax.nn.gelu(dense_pre).astype(bf16)
    dense_pair = near_sum(row_parts(matmul(dense_hidden, dense_down).astype(bf16), 0))
    dense_sum = far_sum(dense_pair)
    far_proj1 = far(attn_proj[1], dense_sum)
    half = expert_up.shape[1] // 2
    far_ex_up = far(expert_up[0, :half], far_proj1)
    stream2 = stream1 + dense_sum.astype(f32)
    qkv1 = jnp.concatenate(near(qkv_t[1], far_qkv1), axis=1)
    proj1 = jnp.concatenate(near(attn_proj[1], far_proj1), axis=0)
    stream3, attn1_state = attention_forward(stream2, norm_gains[1, 0], qkv1, proj1)

    stream3, cot_in, far_ex_up = join(stream3, cot_in, far_ex_up)
    normed, unit_rows, inverse = norm_forward(stream3, norm_gains[1, 1])
    normed_b = normed.astype(bf16)
    far_normed = far(normed_b)
    logits = jnp.dot(normed_b.astype(f32), router_weight, precision=highest)
    gate_probs = jax.nn.softmax(logits, axis=-1)
    gate_all = jnp.stack(gather(gate_probs.T))
    routes_rel = blocked(expert_routes)
    expert_ids = jnp.arange(experts, dtype=jnp.int32)
    gates = jnp.sum(
        jnp.where(routes_rel[:, :, None] == expert_ids[:, None], gate_all[None], 0.0), axis=2
    ).reshape(2, ranks * block)
    gate_slot = jnp.sum(
        jnp.where(first, gates[0], 0.0) + jnp.where(second, gates[1], 0.0), axis=1
    )
    parts, left = [], gate_slot
    for _ in range(3):
        parts.append(lax.optimization_barrier(left.astype(bf16)))
        left = left - parts[-1].astype(f32)
    far_ex_up_rest = far(expert_up[0, half:], far_normed)
    far_normed, gate_slot, parts = join(far_normed, gate_slot, parts)
    normed_all = jnp.concatenate(near(normed_b, far_normed), axis=0)
    far_ex_down = far(expert_down[0], far_ex_up_rest)
    far_ex_up = jnp.concatenate([far_ex_up, far_ex_up_rest], axis=0)
    send = matmul(pick, normed_all).astype(bf16).reshape(experts, room, width)
    row = jnp.arange(room, dtype=jnp.int32)[:, None]
    for at, part in enumerate(parts):
        lanes = jnp.pad(part.reshape(experts, 1, room), ((0, 0), (0, 0), (0, width - room)))
        send = jnp.where(row == quota + at, lanes, send)
    rows_in = all_to_all(send.reshape(slots, width))
    ex_up = jnp.concatenate(near(expert_up[0], far_ex_up), axis=1)
    rows_in, ex_up = join(rows_in, ex_up)
    ex_down = jnp.concatenate(near(expert_down[0], far_ex_down), axis=0)
    gate_rows = rows_in.reshape(experts, room, width)[:, quota : quota + 3, :room]
    gate_in = jnp.sum(gate_rows.astype(f32), axis=1).reshape(slots, 1)
    grad_rows = (gate_in * cot_in.astype(f32)).astype(bf16)

    hidden_pre = matmul(rows_in, ex_up)
    hidden_b = jax.nn.gelu(hidden_pre).astype(bf16)
    send_out = matmul(hidden_b, ex_down).astype(bf16)
    rows_out = all_to_all(send_out)
    unused_out, gelu_back = jax.vjp(jax.nn.gelu, hidden_pre)
    grad_pre = gelu_back(matmul_nt(grad_rows, ex_down))[0].astype(bf16)
    late_rows = after(grad_rows, send_out)
    down_pair = near_sum(row_parts(matmul_tn(hidden_b, late_rows).astype(bf16), 0))
    grad_pre, rows_out, down_pair = join(grad_pre, rows_out, down_pair)
    send_back = matmul_nt(grad_pre, ex_up).astype(bf16)
    grad_ex_down = far_sum(down_pair)
    send_back, grad_pre = join(send_back, grad_pre)
    grad_back = all_to_all(send_back)
    grad_pre, grad_ex_down = join(grad_pre, grad_ex_down)
    up_pair = near_sum(row_parts(matmul_tn(rows_in, grad_pre).astype(bf16), 1))

    out_f = rows_out.astype(f32)
    gate_grad_slot = jnp.sum(cot_slot * out_f, axis=1)
    branch = matmul_tn(pick, (gate_slot[:, None] * out_f).astype(bf16)).astype(bf16)

    own_holder = blocked(holder)[:, 0]
    own_place = blocked(place)[:, 0]
    own_routes = blocked(expert_routes)[:, 0]
    grad_gates = 0.0
    for one, values in zip(order, gather(gate_grad_slot)):
        here = jnp.where(own_holder == one, own_place, -1)
        found = here[..., None] == jnp.arange(slots, dtype=jnp.int32)
        grad_gates = grad_gates + jnp.sum(jnp.where(found, values, 0.0), axis=-1)
    grad_probs = jnp.sum(
        jnp.where(own_routes[..., None] == expert_ids, grad_gates[..., None], 0.0), axis=0
    )
    grad_logits = gate_probs * (
        grad_probs - jnp.sum(gate_probs * grad_probs, axis=-1, keepdims=True)
    )
    grad_router = jnp.dot(normed_b.astype(f32).T, grad_logits, precision=highest)
    grad_back, grad_logits, branch, ex_up_pair = join(grad_back, grad_logits, branch, up_pair)
    grad_branch = matmul_tn(pick, grad_back).astype(bf16)
    grad_normed = far_sum(near_sum(row_parts(grad_branch, 0)))
    grad_normed = grad_normed.astype(f32) + jnp.dot(grad_logits, router_weight.T, precision=highest)
    grad_in, gain_expert = norm_backward(grad_normed, norm_gains[1, 1], unit_rows, inverse)
    grad3 = grad_out + grad_in

    def small_sum(values):
        values = values.astype(bf16)
        values = add_rounded(values, flip(values, 1))
        return add_rounded(values, flip(values, 2))

    def own_pair(*grads):
        pairs = [near_sum(row_parts(one, axis)) for one, axis in grads]
        return tuple(
            jnp.concatenate([one.reshape(-1, width) for one in side], axis=0)
            for side in zip(*pairs)
        )

    order_a = bits
    order_b = [bits[1], bits[0]] + bits[2:]

    def halve_both(pair, step):
        return (dp_halve(pair[0], order_a[step]), dp_halve(pair[1], order_b[step]))

    def double_both(pair, step):
        return (dp_double(pair[0], order_a[step]), dp_double(pair[1], order_b[step]))

    last = len(bits) - 1
    grad2, grad_qkv1, grad_proj1, gain_attn1 = attention_backward(
        grad3, norm_gains[1, 0], qkv1, proj1, attn1_state
    )
    grad2_b = grad2.astype(bf16)
    far_grad2 = far(grad2_b)
    attn1_pair = own_pair((grad_qkv1, 1), (grad_proj1, 0))
    far_grad2, attn1_pair = join(far_grad2, attn1_pair)
    grad2_all = jnp.concatenate(near(grad2_b, far_grad2), axis=0)
    unused_out, gelu_back = jax.vjp(jax.nn.gelu, dense_pre)
    dense_grad = gelu_back(matmul_nt(grad2_all, dense_down))[0].astype(bf16)
    dense_grad_pair = near_sum(row_parts(matmul_nt(dense_grad, dense_up).astype(bf16), 0))
    branch_sum = far_sum(near_sum(row_parts(branch, 0)), far_grad2)
    dense_grad_pair, branch_sum = join(dense_grad_pair, branch_sum)
    grad_normed_m = far_sum(dense_grad_pair)
    attn1_sum = far_sum(attn1_pair, grad_normed_m)
    grad_up = matmul_tn(normed_m, dense_grad).astype(bf16)
    grad_down = matmul_tn(dense_hidden, grad2_all).astype(bf16)
    grad_normed_m, grad_up, grad_down = join(grad_normed_m, grad_up, grad_down)
    dense_parts = halve_both((dp_rows(grad_up), dp_rows(grad_down)), 0)
    grad_in, gain_dense = norm_backward(
        grad_normed_m.astype(f32), norm_gains[0, 1], dense_unit, dense_inverse
    )
    grad1 = grad2 + grad_in

    def between(values):
        nonlocal dense_parts
        values, dense_parts = join(values, dense_parts)
        dense_parts = halve_both(dense_parts, 1)
        return values

    grad0, grad_qkv0, grad_proj0, gain_attn0 = attention_backward(
        grad1, norm_gains[0, 0], qkv0, proj0, attn0_state, between
    )
    attn0_pair = own_pair((grad_qkv0, 1), (grad_proj0, 0))
    smalls = small_sum(
        jnp.concatenate(
            [gain_attn0[None], gain_dense[None], gain_attn1[None], gain_expert[None], grad_router.T],
            axis=0,
        )
    )
    grad0, dense_parts, attn1_sum, attn0_pair, smalls = join(
        grad0, dense_parts, attn1_sum, attn0_pair, smalls
    )
    attn0_sum = far_sum(attn0_pair)

    def in_halves(rows):
        half = rows.shape[0] // 2
        return (rows[:half], rows[half:])

    def advance(parts, at):
        if at <= last:
            return halve_both(parts, at)
        if at <= 2 * last + 1:
            return double_both(parts, 2 * last + 1 - at)
        return parts

    attn1_parts = in_halves(dp_rows(attn1_sum))
    for at in range(2):
        dense_parts = advance(dense_parts, at + 2)
        attn1_parts = advance(attn1_parts, at)
        dense_parts, attn1_parts = join(dense_parts, attn1_parts)
    dense_parts, attn1_parts, attn0_sum = join(dense_parts, attn1_parts, attn0_sum)
    attn0_parts = in_halves(dp_rows(attn0_sum, smalls))
    grad0_b = grad0.astype(bf16)
    stream4 = (stream3 + branch_sum.astype(f32)).astype(bf16)
    ex_up_mine, ex_up_other = ex_up_pair
    split = ex_up_other.shape[0] // 2
    moves = [grad0_b, stream4, ex_up_other[:split], ex_up_other[split:]]
    moved = []
    near_blocks = ()
    ready = ()
    for at in range(2 * last + 2):
        dense_parts = advance(dense_parts, at + 4)
        attn1_parts = advance(attn1_parts, at + 2)
        attn0_parts = advance(attn0_parts, at)
        if at < len(moves):
            moved.append(far(after(moves[at], attn0_sum)))
        if at == 2 * last:
            near_blocks = (near(moves[0], moved[0]), near(moves[1], moved[1]))
        if at == 2 * last + 1:
            ready = (
                in_order(near_blocks[0], me).astype(f32),
                in_order(near_blocks[1], me),
                dense_parts[0][: dense_up.shape[0]].astype(f32),
                dense_parts[1][: dense_down.shape[0]].astype(f32),
            )
        dense_parts, attn1_parts, attn0_parts, moved, near_blocks, ready = join(
            dense_parts, attn1_parts, attn0_parts, moved, near_blocks, ready
        )
        attn0_sum = moved[-1]
    input_grad, block_output, dense_up_sum, dense_down_sum = ready
    grad_ex_up = add_rounded(ex_up_mine, jnp.concatenate(moved[2:], axis=0))
    sums0 = jnp.concatenate(attn0_parts, axis=0).astype(f32)
    sums1 = jnp.concatenate(attn1_parts, axis=0).astype(f32)

    grad_qkv = jnp.stack(
        [
            jnp.swapaxes(sums[: 3 * columns].reshape(3, columns, width), 1, 2)
            for sums in (sums0, sums1)
        ]
    )
    grad_proj = jnp.stack([sums[3 * columns : 4 * columns] for sums in (sums0, sums1)])
    smalls = sums0[4 * columns :]
    grad_gains = smalls[:4].reshape(2, 2, width)
    router_grad = smalls[4 : 4 + experts].T
    return (
        block_output,
        input_grad,
        grad_gains,
        grad_qkv,
        grad_proj,
        dense_up_sum,
        dense_down_sum,
        router_grad,
        grad_ex_up.astype(f32)[None],
        grad_ex_down.astype(f32)[None],
    )


def solution(mesh):
    return jax.shard_map(
        on_device,
        mesh=mesh,
        in_specs=(
            P("dp", None),
            P("dp"),
            P("dp", None),
            P("dp", None),
            P(),
            P(None, None, None, "tensor"),
            P(None, "tensor", None),
            P(None, "tensor"),
            P("tensor", None),
            P(),
            P("dp", None, "tensor"),
            P("dp", "tensor", None),
        ),
        out_specs=(
            P("dp", None),
            P("dp", None),
            P(),
            P(None, None, None, "tensor"),
            P(None, "tensor", None),
            P(None, "tensor"),
            P("tensor", None),
            P(),
            P("dp", None, "tensor"),
            P("dp", "tensor", None),
        ),
        check_vma=False,
    )
```
